512 devices in a mesh: row: 16 (over x_lo, z), col: 8 (over y), depth: 4 (over x_hi, core).
Axes of the slice: x: 4 (x_hi: 2, x_lo: 2; x = x_hi * 2 + x_lo), y: 8, z: 8, core: 2. Of those that a mesh axis runs over, the one named last changes fastest.
Arguments:
- left_blocks: bfloat16 [4, 128, 16, 1, 128, 128], P('depth', 'col', 'row'), may hold values from -0.5 to 0.5
- left_rows: int32 [4, 128, 16, 1], P('depth', 'col', 'row'), may hold values from 0 to 3
- right_blocks: bfloat16 [4, 128, 8, 3, 128, 128], P('depth', 'row', 'col'), may hold values from -0.75 to 0.75
- right_cols: int32 [4, 128, 8, 3], P('depth', 'row', 'col'), may hold values from 0 to 5, all different within a row
Outputs:
- product: float32 [8192, 6144], P(('row', 'depth'), 'col')
The draws below stay inside these ranges and needn't reach their ends.
Inputs may be any that keep to these rules, and one draw needn't show every extreme that they name: For each d, k and r the 1 entries left_rows[d, k, r, :] are distinct. For each d, k and c the 3 entries right_cols[d, k, c, :] are distinct.
All inputs are finite; a program needn't handle non-finite values.
Results may differ from the reference program's by a relative error of at most 0.0003.
Values may be sent and summed in bfloat16 or wider, within the bound.
No kernel may reach another device: no remote copies, remote signals or barrier semaphores. Data moves between devices by JAX's collectives and lax.ppermute only.
A program may use at most 64 MiB of HBM per device.

```python
import jax
import jax.numpy as jnp
from jax import lax

BLOCK = 128
NB = 512
BR = 4
BC = 6
EA = 1
EB = 3
KLAYER = 128
ROWS = 64
COLS = 48
N_ROW = 16
N_COL = 8
N_DEPTH = 4


def steps_of(stream_key, extent, pieces, low, top_value):
    factor_of = 1.0
    for position, blocks in pieces:
        steps = jax.random.uniform(jax.random.fold_in(jax.random.fold_in(stream_key, 6), position), (blocks,), jnp.float32, low / len(pieces), top_value / len(pieces))
        factor_of = factor_of * jnp.repeat(jnp.exp(steps), extent[position] // blocks).reshape((-1,) + (1,) * (len(extent) - 1 - position))
    return factor_of


def picks_of(rng, rows, count, top, lift):
    order = jax.random.permutation(jax.random.fold_in(rng, 1), count)
    pull = order
    for power in range(3):
        pull = pull * pull // count
    pull = pull * lift // count
    chance = jax.random.randint(jax.random.fold_in(rng, 2), (rows, count), 0, 4096) + pull
    fixed_rows = jax.random.permutation(jax.random.fold_in(rng, 3), rows)[jnp.arange(count) % rows]
    chance = jnp.where(jnp.arange(rows)[:, None] == fixed_rows[None, :], 1 << 14, chance)
    merit = chance * count + jnp.arange(count)
    return lax.top_k(merit.astype(jnp.int32), top)[1].astype(jnp.int32)


def normal_values(stream_key, shape, scale, most, shards=(), held_as=jnp.bfloat16):
    entries = scale * jax.random.normal(stream_key, shape, jnp.float32)
    if shards:
        entries = entries * steps_of(stream_key, shape, shards, -0.22, 0.18)
    return jnp.clip(entries, -most, most).astype(held_as)


def setup_inputs(seed: int = 0) -> dict:
    arg_keys = jax.random.split(jax.random.key(seed), 5)
    return {
        "left_blocks": normal_values(arg_keys[0], (N_DEPTH, KLAYER, N_ROW, EA, BLOCK, BLOCK), BLOCK ** -0.5, 0.5, ((0, 4), (1, 8), (2, 16))),
        "left_rows": picks_of(arg_keys[1], N_DEPTH * KLAYER * N_ROW, BR, EA, 0).reshape((N_DEPTH, KLAYER, N_ROW, EA)),
        "right_blocks": normal_values(arg_keys[2], (N_DEPTH, KLAYER, N_COL, EB, BLOCK, BLOCK), (NB * EA * EB // (BR * BC)) ** -0.5, 0.75, ((0, 4), (1, 16), (2, 8))),
        "right_cols": picks_of(arg_keys[3], N_DEPTH * KLAYER * N_COL, BC, EB, 0).reshape((N_DEPTH, KLAYER, N_COL, EB)),
    }


def reference(left_blocks, left_rows, right_blocks, right_cols):
    left_flat = left_blocks.reshape(NB, N_ROW * EA, BLOCK, BLOCK)
    right_flat = right_blocks.reshape(NB, N_COL * EB, BLOCK, BLOCK)
    row_ids = (left_rows + BR * jnp.arange(N_ROW, dtype=jnp.int32)[None, None, :, None]).astype(jnp.int32)
    row_ids = row_ids.reshape(NB, N_ROW * EA)
    col_ids = (right_cols + BC * jnp.arange(N_COL, dtype=jnp.int32)[None, None, :, None]).astype(jnp.int32)
    col_ids = col_ids.reshape(NB, N_COL * EB)

    def step(running, items):
        left_one, right_one, rows_one, cols_one = items
        products = jnp.einsum('axy,byz->abxz', left_one.astype(jnp.float32), right_one.astype(jnp.float32),
                              precision=lax.Precision.HIGHEST)
        running = running.at[rows_one[:, None], cols_one[None, :]].add(products)
        return running, None

    start = jnp.zeros((ROWS, COLS, BLOCK, BLOCK), jnp.float32)
    running, _ = lax.scan(step, start, (left_flat, right_flat, row_ids, col_ids))
    return running.transpose(0, 2, 1, 3).reshape(ROWS * BLOCK, COLS * BLOCK)
```

```python
import jax
import jax.numpy as jnp
from jax import lax
from jax.experimental import pallas as pl
from jax.experimental.pallas import tpu as pltpu
from jax.sharding import PartitionSpec as P

BR = 4
EB = 3
W = 128
NZ = 8
GROUP = 8
PAD = 16
PARTS = ((4, 4, 3), (4, 3, 4))


def zig(z):
    return ((z + 1) // 2) % 2


def ring_pairs(step):
    pairs = []
    for x_lo in range(2):
        for z in range(NZ):
            to = (z + step) % NZ
            pairs.append((x_lo * NZ + z, (x_lo ^ zig(z) ^ zig(to)) * NZ + to))
    return pairs


def chip_pairs(step):
    pairs = []
    for row in range(16):
        for depth in range(4):
            x = (depth // 2) * 2 + row // NZ
            to = (x + step) % 4
            pairs.append(
                (row * 4 + depth, ((to % 2) * NZ + row % NZ) * 4 + (to // 2) * 2 + depth % 2)
            )
    return pairs


def with_index(blocks, index):
    flat = blocks.reshape(-1, W)
    row = jnp.zeros((PAD, W), flat.dtype)
    row = row.at[0, : index.size].set(index.reshape(-1).astype(flat.dtype))
    return jnp.concatenate([flat, row], axis=0)


def multiply(chunk_sizes, place_ref, cols_ref, slot_ref, *refs):
    n = len(chunk_sizes)
    left_hbm = refs[:2]
    right_hbm = refs[2 : 2 + n]
    keep_hbm, send_hbm = refs[2 + n : 4 + n]
    left_buf, right_buf, acc, left_sem, right_sem, out_sem = refs[4 + n :]
    left_copies = [
        pltpu.make_async_copy(left_hbm[t], left_buf.at[t], left_sem.at[t]) for t in range(2)
    ]
    for copy in left_copies:
        copy.start()
    right_copies = [
        pltpu.make_async_copy(
            right_hbm[c], right_buf.at[c, pl.ds(0, right_hbm[c].shape[0])], right_sem.at[c]
        )
        for c in range(n)
    ]
    for copy in right_copies:
        copy.start()
    acc[...] = jnp.zeros_like(acc)
    for copy in left_copies:
        copy.wait()
    for c, (count, offset) in enumerate(chunk_sizes):
        right_copies[c].wait()
        slot = slot_ref[c]

        def body(j, carry, c=c, offset=offset, slot=slot):
            k = offset + j
            rows = pl.ds(pl.multiple_of(k * W, W), W)
            both = jnp.concatenate(
                [left_buf[0, slot, rows, :], left_buf[1, slot, rows, :]], axis=0
            )
            first = j * (EB * W)
            right = jnp.concatenate(
                [
                    right_buf[c, pl.ds(pl.multiple_of(first + e * W, W), W), :]
                    for e in range(EB)
                ],
                axis=1,
            )
            part = jnp.dot(both, right, preferred_element_type=jnp.float32)
            for e in range(EB):
                col = cols_ref[c, j * EB + e]
                lanes = pl.ds(pl.multiple_of(col * W, W), W)
                for t in range(2):
                    at = place_ref[t, slot * GROUP + k]
                    acc[at, :, lanes] += part[t * W : (t + 1) * W, e * W : (e + 1) * W]
            return carry

        lax.fori_loop(0, count, body, 0, unroll=True)
    keep = pltpu.make_async_copy(acc.at[pl.ds(0, 4)], keep_hbm, out_sem.at[0])
    send = pltpu.make_async_copy(acc.at[pl.ds(4, 4)], send_hbm, out_sem.at[1])
    keep.start()
    send.start()
    keep.wait()
    send.wait()


def per_device(left_blocks, left_rows, right_blocks, right_cols):
    row = lax.axis_index("row")
    y = lax.axis_index("col")
    depth = lax.axis_index("depth")
    x_lo, z = row // NZ, row % NZ
    x_hi, core = depth // 2, depth % 2
    x = x_hi * 2 + x_lo
    half = x_lo ^ zig(z)

    left = left_blocks.reshape(2, GROUP * W, W)
    rows = left_rows.reshape(2, GROUP)
    own = (half + y // 4 + y % 4) % 2
    mine = with_index(
        lax.dynamic_index_in_dim(left, own, 0, False),
        lax.dynamic_index_in_dim(rows, own, 0, False),
    )
    other = with_index(
        lax.dynamic_index_in_dim(left, 1 - own, 0, False),
        lax.dynamic_index_in_dim(rows, 1 - own, 0, False),
    )
    right = right_blocks.reshape(GROUP, EB * W, W)
    cols = right_cols.reshape(GROUP, EB)

    left_own = lax.all_gather(mine, "col", axis=0)
    swapped = lax.ppermute(other, "row", [(r, (r + NZ) % 16) for r in range(16)])
    left_other = lax.all_gather(swapped, "col", axis=0)

    chunks, sizes, sources = [], [], []
    streams = []
    offset = 0
    for count, up, down in PARTS:
        part = with_index(right[offset : offset + count], cols[offset : offset + count])
        chunks.append(part)
        sizes.append((count, offset))
        sources.append(z)
        streams.append([part, 1, up, count, offset])
        streams.append([part, -1, down, count, offset])
        offset += count
    for t in range(1, NZ):
        for stream in streams:
            if t <= stream[2]:
                stream[0] = lax.ppermute(stream[0], "row", ring_pairs(stream[1]))
                chunks.append(stream[0])
                sizes.append((stream[3], stream[4]))
                sources.append((z - stream[1] * t) % NZ)
    source = jnp.stack(sources)
    slots = (4 * (zig(source) ^ half) + source // 2).astype(jnp.int32)

    def places(gathered, tile):
        block_row = gathered[:, GROUP * W, :GROUP].astype(jnp.int32)
        ahead = ((block_row // 2) * 2 + tile - x) % 4
        return (((block_row % 2) ^ core) * 4 + ahead).reshape(-1)

    place = jnp.stack([places(left_own, x_lo), places(left_other, 1 - x_lo)])
    most = max(count for count, _ in sizes)
    col_ids = jnp.stack(
        [
            jnp.pad(
                chunk[count * EB * W, : count * EB].astype(jnp.int32),
                (0, (most - count) * EB),
            )
            for chunk, (count, _) in zip(chunks, sizes)
        ]
    )
    n = len(chunks)
    longest = max(chunk.shape[0] for chunk in chunks)
    flops = 2 * 2 * EB * 64 * W**3
    smem = pl.BlockSpec(memory_space=pltpu.SMEM)
    hbm = pl.BlockSpec(memory_space=pl.ANY)
    keep, send = pl.pallas_call(
        lambda *refs: multiply(sizes, *refs),
        out_shape=[jax.ShapeDtypeStruct((4, W, 6 * W), jnp.float32)] * 2,
        in_specs=[smem] * 3 + [hbm] * (2 + n),
        out_specs=[hbm] * 2,
        scratch_shapes=[
            pltpu.VMEM((2, NZ, GROUP * W + PAD, W), jnp.bfloat16),
            pltpu.VMEM((n, longest, W), jnp.bfloat16),
            pltpu.VMEM((8, W, 6 * W), jnp.float32),
            pltpu.SemaphoreType.DMA((2,)),
            pltpu.SemaphoreType.DMA((n,)),
            pltpu.SemaphoreType.DMA((2,)),
        ],
        compiler_params=pltpu.CompilerParams(vmem_limit_bytes=40 * 2**20),
        cost_estimate=pl.CostEstimate(
            flops=flops, bytes_accessed=14 * 2**20, transcendentals=0
        ),
    )(place, col_ids, slots, left_own, left_other, *chunks)
    got = lax.ppermute(send, "depth", [(0, 1), (1, 0), (2, 3), (3, 2)])
    total = keep + got
    out = total[0]
    for step in (2, 1, 3):
        out = out + lax.ppermute(total[step], ("row", "depth"), chip_pairs(step))
    return out


def solution(mesh):
    placed = (
        P("depth", "col", "row", None, None, None),
        P("depth", "col", "row", None),
        P("depth", "row", "col", None, None, None),
        P("depth", "row", "col", None),
    )
    return jax.shard_map(
        per_device,
        mesh=mesh,
        in_specs=placed,
        out_specs=P(("row", "depth"), "col"),
        check_vma=False,
    )
```

```python
import jax
import jax.numpy as jnp
from jax import lax
from jax.experimental import pallas as pl
from jax.experimental.pallas import tpu as pltpu
from jax.sharding import PartitionSpec as P

BR = 4
EB = 3
W = 128
NZ = 8
GROUP = 8
VMEM_LIMIT = 56 * 2**20
PAD = 16
PARTS = ((4, 4, 3), (4, 3, 4))


def zig(z):
    return ((z + 1) // 2) % 2


def ring_pairs(step):
    pairs = []
    for x_lo in range(2):
        for z in range(NZ):
            to = (z + step) % NZ
            pairs.append((x_lo * NZ + z, (x_lo ^ zig(z) ^ zig(to)) * NZ + to))
    return pairs


def with_index(blocks, index):
    flat = blocks.reshape(-1, W)
    row = jnp.zeros((PAD, W), flat.dtype)
    row = row.at[0, : index.size].set(index.reshape(-1).astype(flat.dtype))
    return jnp.concatenate([flat, row], axis=0)


def multiply(chunk_sizes, place_ref, cols_ref, slot_ref, *refs):
    n = len(chunk_sizes)
    left_hbm = refs[0]
    right_hbm = refs[1 : 1 + n]
    keep_hbm, send_hbm = refs[1 + n : 3 + n]
    left_buf, right_buf, acc, left_sem, right_sem, out_sem = refs[3 + n :]
    left_copy = pltpu.make_async_copy(left_hbm, left_buf, left_sem.at[0])
    left_copy.start()
    right_copies = [
        pltpu.make_async_copy(
            right_hbm[c], right_buf.at[c, pl.ds(0, right_hbm[c].shape[0])], right_sem.at[c]
        )
        for c in range(n)
    ]
    for copy in right_copies:
        copy.start()
    acc[...] = jnp.zeros_like(acc)
    left_copy.wait()
    for c, (count, offset) in enumerate(chunk_sizes):
        right_copies[c].wait()
        slot = slot_ref[c]

        def body(j, carry, c=c, offset=offset, slot=slot):
            k = offset + j
            rows = pl.ds(pl.multiple_of(k * W, W), W)
            both = jnp.concatenate(
                [left_buf[slot, 0, rows, :], left_buf[slot, 1, rows, :]], axis=0
            )
            first = j * (EB * W)
            right = jnp.concatenate(
                [
                    right_buf[c, pl.ds(pl.multiple_of(first + e * W, W), W), :]
                    for e in range(EB)
                ],
                axis=1,
            )
            part = jnp.dot(both, right, preferred_element_type=jnp.float32)
            for e in range(EB):
                col = cols_ref[c, j * EB + e]
                lanes = pl.ds(pl.multiple_of(col * W, W), W)
                for t in range(2):
                    at = place_ref[t, slot * GROUP + k]
                    acc[at, :, lanes] += part[t * W : (t + 1) * W, e * W : (e + 1) * W]
            return carry

        lax.fori_loop(0, count, body, 0, unroll=True)
    keep = pltpu.make_async_copy(acc.at[pl.ds(0, 4)], keep_hbm, out_sem.at[0])
    send = pltpu.make_async_copy(acc.at[pl.ds(4, 4)], send_hbm, out_sem.at[1])
    keep.start()
    send.start()
    keep.wait()
    send.wait()


def per_device(left_blocks, left_rows, right_blocks, right_cols):
    x_lo = lax.axis_index("x_lo")
    z = lax.axis_index("z")
    y = lax.axis_index("y")
    core = lax.axis_index("core")
    half = x_lo ^ zig(z)

    left = left_blocks.reshape(2, GROUP * W, W)
    rows = left_rows.reshape(2, GROUP)
    own = (half + y // 4 + y % 4) % 2
    mine = with_index(
        lax.dynamic_index_in_dim(left, own, 0, False),
        lax.dynamic_index_in_dim(rows, own, 0, False),
    )
    other = with_index(
        lax.dynamic_index_in_dim(left, 1 - own, 0, False),
        lax.dynamic_index_in_dim(rows, 1 - own, 0, False),
    )
    right = right_blocks.reshape(GROUP, EB * W, W)
    cols = right_cols.reshape(GROUP, EB)

    swapped = lax.ppermute(other, "x_lo", [(0, 1), (1, 0)])

    chunks, sizes, sources = [], [], []
    streams = []
    offset = 0
    for count, up, down in PARTS:
        part = with_index(right[offset : offset + count], cols[offset : offset + count])
        chunks.append(part)
        sizes.append((count, offset))
        sources.append(z)
        streams.append([part, 1, up, count, offset])
        streams.append([part, -1, down, count, offset])
        offset += count
    for t in range(1, NZ):
        for stream in streams:
            if t <= stream[2]:
                stream[0] = lax.ppermute(stream[0], ("x_lo", "z"), ring_pairs(stream[1]))
                chunks.append(stream[0])
                sizes.append((stream[3], stream[4]))
                sources.append((z - stream[1] * t) % NZ)
    pair = jnp.stack([mine, swapped])
    pair = lax.optimization_barrier((pair, *chunks[len(PARTS) : len(PARTS) + 2]))[0]
    left_all = lax.all_gather(pair, "y", axis=0)
    source = jnp.stack(sources)
    slots = (4 * (zig(source) ^ half) + source // 2).astype(jnp.int32)

    block_row = left_all[:, :, GROUP * W, :GROUP].astype(jnp.int32)
    tile = jnp.stack([x_lo, 1 - x_lo])[None, :, None]
    place = ((block_row % 2) ^ core) * 4 + tile * 2 + block_row // 2
    place = place.transpose(1, 0, 2).reshape(2, NZ * GROUP)
    most = max(count for count, _ in sizes)
    col_ids = jnp.stack(
        [
            jnp.pad(
                chunk[count * EB * W, : count * EB].astype(jnp.int32),
                (0, (most - count) * EB),
            )
            for chunk, (count, _) in zip(chunks, sizes)
        ]
    )
    n = len(chunks)
    longest = max(chunk.shape[0] for chunk in chunks)
    flops = 2 * 2 * EB * 64 * W**3
    smem = pl.BlockSpec(memory_space=pltpu.SMEM)
    hbm = pl.BlockSpec(memory_space=pl.ANY)
    keep, send = pl.pallas_call(
        lambda *refs: multiply(sizes, *refs),
        out_shape=[jax.ShapeDtypeStruct((4, W, 6 * W), jnp.float32)] * 2,
        in_specs=[smem] * 3 + [hbm] * (1 + n),
        out_specs=[hbm] * 2,
        scratch_shapes=[
            pltpu.VMEM((NZ, 2, GROUP * W + PAD, W), jnp.bfloat16),
            pltpu.VMEM((n, longest, W), jnp.bfloat16),
            pltpu.VMEM((8, W, 6 * W), jnp.float32),
            pltpu.SemaphoreType.DMA((1,)),
            pltpu.SemaphoreType.DMA((n,)),
            pltpu.SemaphoreType.DMA((2,)),
        ],
        compiler_params=pltpu.CompilerParams(vmem_limit_bytes=VMEM_LIMIT),
        cost_estimate=pl.CostEstimate(
            flops=flops, bytes_accessed=14 * 2**20, transcendentals=0
        ),
    )(place, col_ids, slots, left_all, *chunks)
    got = lax.ppermute(send, "core", [(0, 1), (1, 0)])
    total = keep + got
    return lax.all_to_all(total, ("x_lo", "x_hi"), 0, 0, tiled=True).sum(0)


def solution(mesh):
    split = jax.sharding.Mesh(
        mesh.devices.reshape(2, NZ, 8, 2, 2), ("x_lo", "z", "y", "x_hi", "core")
    )
    row, depth = ("x_lo", "z"), ("x_hi", "core")
    placed = (
        P(depth, "y", row, None, None, None),
        P(depth, "y", row, None),
        P(depth, row, "y", None, None, None),
        P(depth, row, "y", None),
    )
    return jax.shard_map(
        per_device,
        mesh=split,
        in_specs=placed,
        out_specs=P(row + depth, "y"),
        check_vma=False,
    )
```

```python
import jax
import jax.numpy as jnp
from jax import lax
from jax.experimental import pallas as pl
from jax.experimental.pallas import tpu as pltpu
from jax.sharding import PartitionSpec as P

BR = 4
EB = 3
W = 128
NZ = 8
NY = 8
GROUP = 8
HALF = GROUP // 2
PAD = 16
LPART = GROUP * W + PAD
RPART = HALF * EB * W + PAD
CELL = 6 * W
VMEM_LIMIT = 10 * 2**20


def zig(z):
    return ((z + 1) // 2) % 2


def ring_pairs(step):
    pairs = []
    for x_lo in range(2):
        for z in range(NZ):
            to = (z + step) % NZ
            pairs.append((x_lo * NZ + z, (x_lo ^ zig(z) ^ zig(to)) * NZ + to))
    return pairs


def turn(step):
    return [(y, (y + step) % NY) for y in range(NY)]


def with_index(blocks, index):
    flat = blocks.reshape(-1, W)
    row = jnp.zeros((PAD, W), flat.dtype)
    row = row.at[0, : index.size].set(index.reshape(-1).astype(flat.dtype))
    return jnp.concatenate([flat, row], axis=0)


def load_index(meta, left, slots, held, halves, idx_v, idx_s, sem):
    core, x_lo = meta[0], meta[1]

    def first(ref_rows):
        return ref_rows.astype(jnp.float32)[0:1].astype(jnp.int32)

    for slot in slots:
        for p in range(2):
            rho = first(left[slot, pl.ds(p * LPART + GROUP * W, PAD), :])
            tile = x_lo if p == 0 else 1 - x_lo
            place = ((rho & 1) ^ core) * 4 + tile * 2 + (rho >> 1)
            idx_v[pl.ds(slot * 2 + p, 1), :] = place
    for i, (b, start, _) in enumerate(halves):
        idx_v[pl.ds(2 * NY + i, 1), :] = first(held[b, pl.ds(start + HALF * EB * W, PAD), :])
    copy = pltpu.make_async_copy(idx_v, idx_s, sem)
    copy.start()
    copy.wait()


def add_half(left, acc, idx_s, i, held, entry, slot):
    b, start, half = entry
    for j in range(HALF):
        k = half * HALF + j
        both = jnp.concatenate(
            [left[slot, pl.ds(p * LPART + k * W, W), :] for p in range(2)], axis=0
        )
        right = jnp.concatenate(
            [held[b, pl.ds(start + (j * EB + e) * W, W), :] for e in range(EB)], axis=1
        )
        part = jnp.dot(both, right, preferred_element_type=jnp.float32)
        for e in range(EB):
            lanes = pl.ds(pl.multiple_of(idx_s[2 * NY + i, j * EB + e] * W, W), W)
            for p in range(2):
                at = idx_s[slot * 2 + p, k]
                acc[at, :, lanes] += part[p * W : (p + 1) * W, e * W : (e + 1) * W]


def fetch(pairs, sems):
    copies = [pltpu.make_async_copy(a, b, sems.at[i]) for i, (a, b) in enumerate(pairs)]
    for copy in copies:
        copy.start()
    return copies


def halves_of(count):
    return [(b, h * RPART, h) for b in range(count) for h in range(2)]


def near(meta, *refs):
    lefts, rights, (acc, left, held, idx_v, idx_s, sem, sems) = refs[:7], refs[7:12], refs[12:]
    pairs = [(ref, left.at[slot]) for slot, ref in enumerate(lefts)]
    pairs += [(ref, held.at[b]) for b, ref in enumerate(rights)]
    copies = fetch(pairs, sems)
    acc[...] = jnp.zeros_like(acc)
    for copy in copies:
        copy.wait()
    halves = halves_of(5)
    load_index(meta, left, range(7), held, halves, idx_v, idx_s, sem)
    for c in range(5):

        @pl.when(meta[2 + c] != NY - 1)
        def _(c=c):
            for i in (2 * c, 2 * c + 1):
                add_half(left, acc, idx_s, i, held, halves[i], meta[2 + c])


def mid(meta, *refs):
    lefts, rights, (_, _, acc, left, held, idx_v, idx_s, sem, sems) = refs[:2], refs[2:9], refs[9:]
    pairs = [(ref, left.at[NY - 1, pl.ds(p * LPART, LPART)]) for p, ref in enumerate(lefts)]
    pairs += [(ref, held.at[b]) for b, ref in enumerate(rights[5:])]
    copies = fetch(pairs, sems)
    for c in range(6):
        chosen = meta[10] == 0 if c == 5 else meta[2 + c] == NY - 1

        @pl.when(chosen)
        def _(c=c):
            late = pltpu.make_async_copy(rights[c], held.at[2], sems.at[4])
            late.start()
            late.wait()

    for copy in copies:
        copy.wait()
    halves = halves_of(3)
    load_index(meta, left, range(NY), held, halves, idx_v, idx_s, sem)
    for i in range(4):
        add_half(left, acc, idx_s, i, held, halves[i], meta[7 + i // 2])

    @pl.when(meta[10] != 0)
    def _():
        for i in (4, 5):
            add_half(left, acc, idx_s, i, held, halves[i], NY - 1)


def far(meta, *refs):
    rights, (left, _, acc, held, idx_v, idx_s, sem, sems) = refs[:2], refs[2:]
    copies = fetch([(ref, held.at[b]) for b, ref in enumerate(rights)], sems)
    for copy in copies:
        copy.wait()
    halves = [(h, 0, h) for h in range(2)]
    load_index(meta, left, range(NY), held, halves, idx_v, idx_s, sem)
    for i, entry in enumerate(halves):
        add_half(left, acc, idx_s, i, held, entry, meta[9])


def call(body, meta, operands, near_by, outs, aliases, buffer, blocks):
    smem = pl.BlockSpec(memory_space=pltpu.SMEM)
    vmem = pl.BlockSpec(memory_space=pltpu.VMEM)
    far_off = pl.BlockSpec(memory_space=pl.ANY)
    return pl.pallas_call(
        body,
        out_shape=outs,
        in_specs=[smem] + [far_off] * len(operands) + [vmem] * len(near_by),
        out_specs=[vmem] * len(outs),
        input_output_aliases=aliases,
        scratch_shapes=[
            pltpu.VMEM(buffer, jnp.bfloat16),
            pltpu.VMEM((2 * NY + PAD, W), jnp.int32),
            pltpu.SMEM((2 * NY + PAD, W), jnp.int32),
            pltpu.SemaphoreType.DMA,
            pltpu.SemaphoreType.DMA((12,)),
        ],
        compiler_params=pltpu.CompilerParams(vmem_limit_bytes=VMEM_LIMIT),
        cost_estimate=pl.CostEstimate(
            flops=2 * blocks * W**3, bytes_accessed=2**20, transcendentals=0
        ),
    )(meta, *operands, *near_by)


def per_device(left_blocks, left_rows, right_blocks, right_cols):
    x_lo = lax.axis_index("x_lo")
    z = lax.axis_index("z")
    y = lax.axis_index("y")
    core = lax.axis_index("core")
    side = x_lo ^ zig(z)

    left = left_blocks.reshape(2, GROUP * W, W)
    rows = left_rows.reshape(2, GROUP)
    own = (side + y // 4 + y % 4) % 2

    def group(which):
        return with_index(
            lax.dynamic_index_in_dim(left, which, 0, False),
            lax.dynamic_index_in_dim(rows, which, 0, False),
        )

    swapped = lax.ppermute(group(1 - own), "x_lo", [(0, 1), (1, 0)])
    pair = jnp.concatenate([group(own), swapped], axis=0)
    right = right_blocks.reshape(2, HALF, EB * W, W)
    cols = right_cols.reshape(2, HALF * EB)
    chunk = jnp.concatenate([with_index(right[h], cols[h]) for h in range(2)], axis=0)
    first, _ = lax.optimization_barrier((chunk, swapped))

    row = ("x_lo", "z")
    up = down = first
    fore = back = pair
    rights, lefts = [chunk], [pair]
    for _ in range(3):
        up = lax.ppermute(up, row, ring_pairs(1))
        down = lax.ppermute(down, row, ring_pairs(-1))
        fore = lax.ppermute(fore, "y", turn(1))
        back = lax.ppermute(back, "y", turn(-1))
        rights += [up, down]
        lefts += [fore, back]
    last_left = [
        lax.ppermute(fore[:LPART], "y", turn(1)),
        lax.ppermute(back[LPART:], "y", turn(-1)),
    ]
    last_right = [
        lax.ppermute(up[:RPART], row, ring_pairs(1)),
        lax.ppermute(down[RPART:], row, ring_pairs(-1)),
    ]

    source = (z + jnp.array([0, -1, 1, -2, 2, -3, 3, 4], jnp.int32)) % NZ
    away = (4 * (zig(source) ^ side) + source // 2 - y) % NY
    slot = jnp.where(
        away == 0, 0, jnp.where(away == 4, 7, jnp.where(away < 4, 2 * away, 15 - 2 * away))
    )
    late = (slot[:5] == NY - 1).any()
    meta = jnp.concatenate([jnp.stack([core, x_lo]), slot, late[None]]).astype(jnp.int32)

    sums = jax.ShapeDtypeStruct((8, W, CELL), jnp.float32)
    kept = jax.ShapeDtypeStruct((NY, 2 * LPART, W), jnp.bfloat16)
    chunks = lambda n: (n, 2 * RPART, W)
    acc, left_all = call(near, meta, lefts + rights[:5], [], [sums, kept], {}, chunks(5), 240)
    acc, left_all = call(
        mid,
        meta,
        last_left + rights,
        [acc, left_all],
        [sums, kept],
        {10: 0, 11: 1},
        chunks(3),
        96,
    )
    (acc,) = call(far, meta, last_right, [left_all, acc], [sums], {4: 0}, (2, RPART, W), 48)

    got = lax.ppermute(acc[4:], "core", [(0, 1), (1, 0)])
    total = acc[:4] + got
    return lax.all_to_all(total, ("x_lo", "x_hi"), 0, 0, tiled=True).sum(0)


def solution(mesh):
    split = jax.sharding.Mesh(
        mesh.devices.reshape(2, NZ, NY, 2, 2), ("x_lo", "z", "y", "x_hi", "core")
    )
    row, depth = ("x_lo", "z"), ("x_hi", "core")
    placed = (
        P(depth, "y", row, None, None, None),
        P(depth, "y", row, None),
        P(depth, row, "y", None, None, None),
        P(depth, row, "y", None),
    )
    return jax.shard_map(
        per_device,
        mesh=split,
        in_specs=placed,
        out_specs=P(row + depth, "y"),
        check_vma=False,
    )
```

```python
import jax
import jax.numpy as jnp
from jax import lax
from jax.experimental import pallas as pl
from jax.experimental.pallas import tpu as pltpu
from jax.sharding import PartitionSpec as P

BR = 4
EB = 3
W = 128
NZ = 8
NY = 8
GROUP = 8
HALF = GROUP // 2
PAD = 16
LPART = GROUP * W + PAD
RPART = HALF * EB * W + PAD
CELL = 6 * W
VMEM_LIMIT = 8 * 2**20


def zig(z):
    return ((z + 1) // 2) % 2


def ring_pairs(step):
    pairs = []
    for x_lo in range(2):
        for z in range(NZ):
            to = (z + step) % NZ
            pairs.append((x_lo * NZ + z, (x_lo ^ zig(z) ^ zig(to)) * NZ + to))
    return pairs


def turn(step):
    return [(y, (y + step) % NY) for y in range(NY)]


def with_index(blocks, index):
    flat = blocks.reshape(-1, W)
    row = jnp.zeros((PAD, W), flat.dtype)
    row = row.at[0, : index.size].set(index.reshape(-1).astype(flat.dtype))
    return jnp.concatenate([flat, row], axis=0)


def load_index(meta, left, right, slots, chunks, idx_v, idx_s, sem):
    core, x_lo = meta[0], meta[1]

    def first(ref_rows):
        return ref_rows.astype(jnp.float32)[0:1].astype(jnp.int32)

    for slot in range(slots):
        for p in range(2):
            rho = first(left[slot, pl.ds(p * LPART + GROUP * W, PAD), :])
            tile = x_lo if p == 0 else 1 - x_lo
            place = ((rho & 1) ^ core) * 4 + tile * 2 + (rho >> 1)
            idx_v[pl.ds(slot * 2 + p, 1), :] = place
    for c in range(chunks):
        for h in range(2):
            row = first(right[c, pl.ds(h * RPART + HALF * EB * W, PAD), :])
            idx_v[pl.ds(2 * NY + 2 * c + h, 1), :] = row
    copy = pltpu.make_async_copy(idx_v, idx_s, sem)
    copy.start()
    copy.wait()


def add_chunk(left, right, acc, idx_s, c, slot):
    for k in range(GROUP):
        half, j = k // HALF, k % HALF
        both = jnp.concatenate(
            [left[slot, pl.ds(p * LPART + k * W, W), :] for p in range(2)], axis=0
        )
        wide = jnp.concatenate(
            [right[c, pl.ds(half * RPART + (j * EB + e) * W, W), :] for e in range(EB)], axis=1
        )
        part = jnp.dot(both, wide, preferred_element_type=jnp.float32)
        for e in range(EB):
            cell = idx_s[2 * NY + 2 * c + half, j * EB + e]
            lanes = pl.ds(pl.multiple_of(cell * W, W), W)
            for p in range(2):
                at = idx_s[slot * 2 + p, k]
                acc[at, :, lanes] += part[p * W : (p + 1) * W, e * W : (e + 1) * W]


def stage(number, new_left, new_right, slots, chunks, meta, *refs):
    n, m = len(new_left), len(new_right)
    arrived = refs[: n + m]
    acc, left, right, token, idx_v, idx_s, sem, sems = refs[-8:]
    token[...] = jnp.zeros_like(token)
    targets = [left.at[at, pl.ds(start, size)] for at, start, size in new_left]
    targets += [right.at[at, pl.ds(start, size)] for at, start, size in new_right]
    copies = [
        pltpu.make_async_copy(ref, target, sems.at[i])
        for i, (ref, target) in enumerate(zip(arrived, targets))
    ]
    for copy in copies:
        copy.start()
    if number == 1:
        acc[...] = jnp.zeros_like(acc)
    for copy in copies:
        copy.wait()
    load_index(meta, left, right, slots, chunks, idx_v, idx_s, sem)

    def body(c, carry):
        @pl.when(meta[10 + c] == number)
        def _():
            add_chunk(left, right, acc, idx_s, c, meta[2 + c])

        return carry

    lax.fori_loop(0, chunks, body, 0)


def run_stage(number, meta, lefts, rights, slots, chunks, state, *after):
    new_left = [(at, start, ref.shape[0]) for at, start, ref in lefts]
    new_right = [(at, start, ref.shape[0]) for at, start, ref in rights]
    operands = [ref for _, _, ref in lefts + rights]
    n = len(operands)
    smem = pl.BlockSpec(memory_space=pltpu.SMEM)
    vmem = pl.BlockSpec(memory_space=pltpu.VMEM)
    far_off = pl.BlockSpec(memory_space=pl.ANY)
    return pl.pallas_call(
        lambda *refs: stage(number, new_left, new_right, slots, chunks, *refs),
        out_shape=[
            jax.ShapeDtypeStruct((8, W, CELL), jnp.float32),
            jax.ShapeDtypeStruct((NY, 2 * LPART, W), jnp.bfloat16),
            jax.ShapeDtypeStruct((NZ, 2 * RPART, W), jnp.bfloat16),
            jax.ShapeDtypeStruct((8, W), jnp.int32),
        ],
        in_specs=[smem] + [far_off] * n + [vmem] * len(state) + [far_off] * len(after),
        out_specs=[vmem] * 4,
        input_output_aliases={1 + n + i: i for i in range(len(state))},
        scratch_shapes=[
            pltpu.VMEM((4 * NY, W), jnp.int32),
            pltpu.SMEM((4 * NY, W), jnp.int32),
            pltpu.SemaphoreType.DMA,
            pltpu.SemaphoreType.DMA((8,)),
        ],
        compiler_params=pltpu.CompilerParams(vmem_limit_bytes=VMEM_LIMIT),
        cost_estimate=pl.CostEstimate(
            flops=8 * 48 * W**3, bytes_accessed=2**20, transcendentals=0
        ),
    )(meta, *operands, *state, *after)


def per_device(left_blocks, left_rows, right_blocks, right_cols):
    x_lo = lax.axis_index("x_lo")
    z = lax.axis_index("z")
    y = lax.axis_index("y")
    core = lax.axis_index("core")
    side = x_lo ^ zig(z)

    left = left_blocks.reshape(2, GROUP * W, W)
    rows = left_rows.reshape(2, GROUP)
    own = (side + y // 4 + y % 4) % 2

    def group(which):
        return with_index(
            lax.dynamic_index_in_dim(left, which, 0, False),
            lax.dynamic_index_in_dim(rows, which, 0, False),
        )

    swapped = lax.ppermute(group(1 - own), "x_lo", [(0, 1), (1, 0)])
    pair = jnp.concatenate([group(own), swapped], axis=0)
    right = right_blocks.reshape(2, HALF, EB * W, W)
    cols = right_cols.reshape(2, HALF * EB)
    chunk = jnp.concatenate([with_index(right[h], cols[h]) for h in range(2)], axis=0)
    first, _ = lax.optimization_barrier((chunk, swapped))

    source = (z + jnp.array([0, -1, 1, -2, 2, -3, 3, 4], jnp.int32)) % NZ
    away = (4 * (zig(source) ^ side) + source // 2 - y) % NY
    slot = jnp.where(
        away == 0, 0, jnp.where(away == 4, 7, jnp.where(away < 4, 2 * away, 15 - 2 * away))
    )
    right_at = jnp.array([1, 1, 1, 2, 2, 3, 3, 4], jnp.int32)
    left_at = jnp.where(slot < 3, 1, jnp.where(slot < 5, 2, 3))
    meta = jnp.concatenate([jnp.stack([core, x_lo]), slot, jnp.maximum(right_at, left_at)])
    meta = meta.astype(jnp.int32)

    def listed(arrays, low, high):
        return [(i, 0, arrays[i]) for i in range(low, high)]

    row = ("x_lo", "z")

    def step_z(up, down):
        return lax.ppermute(up, row, ring_pairs(1)), lax.ppermute(down, row, ring_pairs(-1))

    def step_y(fore, back):
        return lax.ppermute(fore, "y", turn(1)), lax.ppermute(back, "y", turn(-1))

    rights = [chunk, *step_z(first, first)]
    lefts = [pair, *step_y(pair, pair)]
    rights += step_z(*rights[1:3])
    lefts += step_y(*lefts[1:3])
    *state, token = run_stage(1, meta, listed(lefts, 0, 3), listed(rights, 0, 3), 3, 3, [])
    up, down, token = lax.optimization_barrier((*rights[3:5], token))
    rights += step_z(up, down)
    lefts += step_y(*lefts[3:5])
    *state, token = run_stage(2, meta, listed(lefts, 3, 5), listed(rights, 3, 5), 5, 5, state, token)
    last_left = step_y(lefts[5][:LPART], lefts[6][LPART:])
    up, down, token, *last_left = lax.optimization_barrier((*rights[5:7], token, *last_left))
    last_right = step_z(up[:RPART], down[RPART:])
    ends = [(7, 0, last_left[0]), (7, LPART, last_left[1])]
    *state, _ = run_stage(3, meta, listed(lefts, 5, 7) + ends, listed(rights, 5, 7), 8, 7, state, token)
    ends = [(7, 0, last_right[0]), (7, RPART, last_right[1])]
    acc = run_stage(4, meta, [], ends, 8, 8, state)[0]

    got = lax.ppermute(acc[4:], "core", [(0, 1), (1, 0)])
    total = acc[:4] + got
    return lax.all_to_all(total, ("x_lo", "x_hi"), 0, 0, tiled=True).sum(0)


def solution(mesh):
    split = jax.sharding.Mesh(
        mesh.devices.reshape(2, NZ, NY, 2, 2), ("x_lo", "z", "y", "x_hi", "core")
    )
    row, depth = ("x_lo", "z"), ("x_hi", "core")
    placed = (
        P(depth, "y", row, None, None, None),
        P(depth, "y", row, None),
        P(depth, row, "y", None, None, None),
        P(depth, row, "y", None),
    )
    return jax.shard_map(
        per_device,
        mesh=split,
        in_specs=placed,
        out_specs=P(row + depth, "y"),
        check_vma=False,
    )
```

```python
import jax
import jax.numpy as jnp
from jax import lax
from jax.experimental import pallas as pl
from jax.experimental.pallas import tpu as pltpu
from jax.sharding import PartitionSpec as P

BR = 4
EB = 3
W = 128
NZ = 8
NY = 8
GROUP = 8
HALF = GROUP // 2
PAD = 16
LPART = GROUP * W + PAD
RPART = HALF * EB * W + PAD
CELL = 6 * W
TOP = 32767.0
VMEM_LIMIT = 8 * 2**20


def zig(z):
    return ((z + 1) // 2) % 2


def ring_pairs(step):
    pairs = []
    for x_lo in range(2):
        for z in range(NZ):
            to = (z + step) % NZ
            pairs.append((x_lo * NZ + z, (x_lo ^ zig(z) ^ zig(to)) * NZ + to))
    return pairs


def turn(step):
    return [(y, (y + step) % NY) for y in range(NY)]


def with_index(blocks, index):
    flat = blocks.reshape(-1, W)
    row = jnp.zeros((PAD, W), flat.dtype)
    row = row.at[0, : index.size].set(index.reshape(-1).astype(flat.dtype))
    return jnp.concatenate([flat, row], axis=0)


def load_index(meta, left, right, slots, chunks, idx_v, idx_s, sem):
    core, x_lo = meta[0], meta[1]

    def first(ref_rows):
        return ref_rows.astype(jnp.float32)[0:1].astype(jnp.int32)

    for i, slot in enumerate(slots):
        for p in range(2):
            rho = first(left[slot, pl.ds(p * LPART + GROUP * W, PAD), :])
            tile = x_lo if p == 0 else 1 - x_lo
            place = ((rho & 1) ^ core) * 4 + tile * 2 + (rho >> 1)
            idx_v[pl.ds(i * 2 + p, 1), :] = place
    for c in chunks:
        for h in range(2):
            row = first(right[c, pl.ds(h * RPART + HALF * EB * W, PAD), :])
            idx_v[pl.ds(2 * NY + 2 * c + h, 1), :] = row
    copy = pltpu.make_async_copy(idx_v, idx_s, sem)
    copy.start()
    copy.wait()


def add_chunk(left, right, acc, idx_s, c, slot, place):
    for k in range(GROUP):
        half, j = k // HALF, k % HALF
        both = jnp.concatenate(
            [left[slot, pl.ds(p * LPART + k * W, W), :] for p in range(2)], axis=0
        )
        wide = jnp.concatenate(
            [right[c, pl.ds(half * RPART + (j * EB + e) * W, W), :] for e in range(EB)], axis=1
        )
        part = jnp.dot(both, wide, preferred_element_type=jnp.float32)
        for e in range(EB):
            cell = idx_s[2 * NY + 2 * c + half, j * EB + e]
            lanes = pl.ds(pl.multiple_of(cell * W, W), W)
            for p in range(2):
                at = idx_s[place * 2 + p, k]
                acc[at, :, lanes] += part[p * W : (p + 1) * W, e * W : (e + 1) * W]


def stage(number, new_left, new_right, slots, chunks, meta, *refs):
    n, m = len(new_left), len(new_right)
    arrived = refs[: n + m]
    acc, left, right, token, idx_v, idx_s, sem, sems = refs[-8:]
    token[...] = jnp.zeros_like(token)
    targets = [left.at[at, pl.ds(start, size)] for at, start, size in new_left]
    targets += [right.at[at, pl.ds(start, size)] for at, start, size in new_right]
    copies = [
        pltpu.make_async_copy(ref, target, sems.at[i])
        for i, (ref, target) in enumerate(zip(arrived, targets))
    ]
    for copy in copies:
        copy.start()
    if number == 1:
        acc[...] = jnp.zeros_like(acc)
    for copy in copies:
        copy.wait()
    if number == 4:
        load_index(meta, left, right, [meta[9]], [7], idx_v, idx_s, sem)
        add_chunk(left, right, acc, idx_s, 7, meta[9], 0)
        return
    load_index(meta, left, right, range(slots), range(chunks), idx_v, idx_s, sem)

    def body(c, carry):
        @pl.when(meta[10 + c] == number)
        def _():
            add_chunk(left, right, acc, idx_s, c, meta[2 + c], meta[2 + c])

        return carry

    lax.fori_loop(0, chunks, body, 0)


def run_stage(number, meta, lefts, rights, slots, chunks, state, *after):
    new_left = [(at, start, ref.shape[0]) for at, start, ref in lefts]
    new_right = [(at, start, ref.shape[0]) for at, start, ref in rights]
    operands = [ref for _, _, ref in lefts + rights]
    n = len(operands)
    smem = pl.BlockSpec(memory_space=pltpu.SMEM)
    vmem = pl.BlockSpec(memory_space=pltpu.VMEM)
    far_off = pl.BlockSpec(memory_space=pl.ANY)
    return pl.pallas_call(
        lambda *refs: stage(number, new_left, new_right, slots, chunks, *refs),
        out_shape=[
            jax.ShapeDtypeStruct((8, W, CELL), jnp.float32),
            jax.ShapeDtypeStruct((NY, 2 * LPART, W), jnp.bfloat16),
            jax.ShapeDtypeStruct((NZ, 2 * RPART, W), jnp.bfloat16),
            jax.ShapeDtypeStruct((8, W), jnp.int32),
        ],
        in_specs=[smem] + [far_off] * n + [vmem] * len(state) + [far_off] * len(after),
        out_specs=[vmem] * 4,
        input_output_aliases={1 + n + i: i for i in range(len(state))},
        scratch_shapes=[
            pltpu.VMEM((4 * NY, W), jnp.int32),
            pltpu.SMEM((4 * NY, W), jnp.int32),
            pltpu.SemaphoreType.DMA,
            pltpu.SemaphoreType.DMA((8,)),
        ],
        compiler_params=pltpu.CompilerParams(vmem_limit_bytes=VMEM_LIMIT),
        cost_estimate=pl.CostEstimate(
            flops=8 * 48 * W**3, bytes_accessed=2**20, transcendentals=0
        ),
    )(meta, *operands, *state, *after)


def encode(total):
    top = jnp.maximum(jnp.abs(total).max(axis=-1, keepdims=True), 2.0**-100)
    power = jnp.ceil(jnp.log2(top))
    whole = jnp.round(total * jnp.exp2(-power) * TOP)
    whole = jnp.clip(whole, -TOP, TOP).astype(jnp.int16)
    power = jnp.broadcast_to(power.astype(jnp.int16), total.shape[:-1] + (W,))
    return jnp.concatenate([whole, power], axis=-1)


def decode(moved):
    power = moved[..., CELL : CELL + 1].astype(jnp.float32)
    return moved[..., :CELL].astype(jnp.float32) * (jnp.exp2(power) / TOP)


def per_device(left_blocks, left_rows, right_blocks, right_cols):
    x_lo = lax.axis_index("x_lo")
    z = lax.axis_index("z")
    y = lax.axis_index("y")
    core = lax.axis_index("core")
    side = x_lo ^ zig(z)

    left = left_blocks.reshape(2, GROUP * W, W)
    rows = left_rows.reshape(2, GROUP)
    own = (side + y // 4 + y % 4) % 2

    def group(which):
        return with_index(
            lax.dynamic_index_in_dim(left, which, 0, False),
            lax.dynamic_index_in_dim(rows, which, 0, False),
        )

    swapped = lax.ppermute(group(1 - own), "x_lo", [(0, 1), (1, 0)])
    pair = jnp.concatenate([group(own), swapped], axis=0)
    right = right_blocks.reshape(2, HALF, EB * W, W)
    cols = right_cols.reshape(2, HALF * EB)
    chunk = jnp.concatenate([with_index(right[h], cols[h]) for h in range(2)], axis=0)
    first = chunk

    source = (z + jnp.array([0, -1, 1, -2, 2, -3, 3, 4], jnp.int32)) % NZ
    away = (4 * (zig(source) ^ side) + source // 2 - y) % NY
    slot = jnp.where(
        away == 0, 0, jnp.where(away == 4, 7, jnp.where(away < 4, 2 * away, 15 - 2 * away))
    )
    right_at = jnp.array([1, 1, 1, 2, 2, 3, 3, 4], jnp.int32)
    left_at = jnp.where(slot < 3, 1, jnp.where(slot < 5, 2, 3))
    meta = jnp.concatenate([jnp.stack([core, x_lo]), slot, jnp.maximum(right_at, left_at)])
    meta = meta.astype(jnp.int32)

    def listed(arrays, low, high):
        return [(i, 0, arrays[i]) for i in range(low, high)]

    row = ("x_lo", "z")

    def step_z(up, down):
        return lax.ppermute(up, row, ring_pairs(1)), lax.ppermute(down, row, ring_pairs(-1))

    def step_y(fore, back):
        return lax.ppermute(fore, "y", turn(1)), lax.ppermute(back, "y", turn(-1))

    rights = [chunk, *step_z(first, first)]
    lefts = [pair, *step_y(pair, pair)]
    rights += step_z(*rights[1:3])
    lefts += step_y(*lefts[1:3])
    *state, token = run_stage(1, meta, listed(lefts, 0, 3), listed(rights, 0, 3), 3, 3, [])
    up, down, token = lax.optimization_barrier((*rights[3:5], token))
    rights += step_z(up, down)
    lefts += step_y(*lefts[3:5])
    *state, token = run_stage(2, meta, listed(lefts, 3, 5), listed(rights, 3, 5), 5, 5, state, token)
    last_left = step_y(lefts[5][:LPART], lefts[6][LPART:])
    up, down, token, *last_left = lax.optimization_barrier((*rights[5:7], token, *last_left))
    last_right = step_z(up[:RPART], down[RPART:])
    ends = [(7, 0, last_left[0]), (7, LPART, last_left[1])]
    *state, _ = run_stage(3, meta, listed(lefts, 5, 7) + ends, listed(rights, 5, 7), 8, 7, state, token)
    ends = [(7, 0, last_right[0]), (7, RPART, last_right[1])]
    acc = run_stage(4, meta, [], ends, 8, 8, state)[0]

    got = lax.ppermute(acc[4:], "core", [(0, 1), (1, 0)])
    total = acc[:4] + got
    moved = lax.all_to_all(encode(total), ("x_lo", "x_hi"), 0, 0, tiled=True)
    return decode(moved).sum(0)


def solution(mesh):
    split = jax.sharding.Mesh(
        mesh.devices.reshape(2, NZ, NY, 2, 2), ("x_lo", "z", "y", "x_hi", "core")
    )
    row, depth = ("x_lo", "z"), ("x_hi", "core")
    placed = (
        P(depth, "y", row, None, None, None),
        P(depth, "y", row, None),
        P(depth, row, "y", None, None, None),
        P(depth, row, "y", None),
    )
    return jax.shard_map(
        per_device,
        mesh=split,
        in_specs=placed,
        out_specs=P(row + depth, "y"),
        check_vma=False,
    )
```

```python
import jax
import jax.numpy as jnp
from jax import lax
from jax.experimental import pallas as pl
from jax.experimental.pallas import tpu as pltpu
from jax.sharding import PartitionSpec as P

BR = 4
EB = 3
W = 128
NZ = 8
NY = 8
GROUP = 8
HALF = GROUP // 2
PAD = 16
LPART = GROUP * W + PAD
RPART = HALF * EB * W + PAD
CELL = 6 * W
TOP = 32767.0
VMEM_LIMIT = 8 * 2**20


def zig(z):
    return ((z + 1) // 2) % 2


def ring_pairs(step):
    pairs = []
    for x_lo in range(2):
        for z in range(NZ):
            to = (z + step) % NZ
            pairs.append((x_lo * NZ + z, (x_lo ^ zig(z) ^ zig(to)) * NZ + to))
    return pairs


def turn(step):
    return [(y, (y + step) % NY) for y in range(NY)]


def chip_pairs(step):
    def other(i):
        return (i % 2) * 2 + i // 2

    return [(i, other((other(i) + step) % 4)) for i in range(4)]


def with_index(blocks, index):
    flat = blocks.reshape(-1, W)
    row = jnp.zeros((PAD, W), flat.dtype)
    row = row.at[0, : index.size].set(index.reshape(-1).astype(flat.dtype))
    return jnp.concatenate([flat, row], axis=0)


def load_index(meta, left, right, slots, chunks, idx_v, idx_s, sem):
    core, x_lo = meta[0], meta[1]

    def first(ref_rows):
        return ref_rows.astype(jnp.float32)[0:1].astype(jnp.int32)

    for i, slot in enumerate(slots):
        for p in range(2):
            rho = first(left[slot, pl.ds(p * LPART + GROUP * W, PAD), :])
            tile = x_lo if p == 0 else 1 - x_lo
            ahead = ((rho >> 1) * 2 + tile - meta[18]) & 3
            place = ((rho & 1) ^ core) * 4 + ahead
            idx_v[pl.ds(i * 2 + p, 1), :] = place
    for c in chunks:
        for h in range(2):
            row = first(right[c, pl.ds(h * RPART + HALF * EB * W, PAD), :])
            idx_v[pl.ds(2 * NY + 2 * c + h, 1), :] = row
    copy = pltpu.make_async_copy(idx_v, idx_s, sem)
    copy.start()
    copy.wait()


def add_chunk(left, right, acc, idx_s, c, slot, place):
    for k in range(GROUP):
        half, j = k // HALF, k % HALF
        both = jnp.concatenate(
            [left[slot, pl.ds(p * LPART + k * W, W), :] for p in range(2)], axis=0
        )
        wide = jnp.concatenate(
            [right[c, pl.ds(half * RPART + (j * EB + e) * W, W), :] for e in range(EB)], axis=1
        )
        part = jnp.dot(both, wide, preferred_element_type=jnp.float32)
        for e in range(EB):
            cell = idx_s[2 * NY + 2 * c + half, j * EB + e]
            lanes = pl.ds(pl.multiple_of(cell * W, W), W)
            for p in range(2):
                at = idx_s[place * 2 + p, k]
                acc[at, :, lanes] += part[p * W : (p + 1) * W, e * W : (e + 1) * W]


def stage(number, new_left, new_right, slots, chunks, meta, *refs):
    n, m = len(new_left), len(new_right)
    arrived = refs[: n + m]
    acc, left, right, token, idx_v, idx_s, sem, sems = refs[-8:]
    token[...] = jnp.zeros_like(token)
    targets = [left.at[at, pl.ds(start, size)] for at, start, size in new_left]
    targets += [right.at[at, pl.ds(start, size)] for at, start, size in new_right]
    copies = [
        pltpu.make_async_copy(ref, target, sems.at[i])
        for i, (ref, target) in enumerate(zip(arrived, targets))
    ]
    for copy in copies:
        copy.start()
    if number == 1:
        acc[...] = jnp.zeros_like(acc)
    for copy in copies:
        copy.wait()
    if number == 4:
        load_index(meta, left, right, [meta[9]], [7], idx_v, idx_s, sem)
        add_chunk(left, right, acc, idx_s, 7, meta[9], 0)
        return
    load_index(meta, left, right, range(slots), range(chunks), idx_v, idx_s, sem)

    def body(c, carry):
        @pl.when(meta[10 + c] == number)
        def _():
            add_chunk(left, right, acc, idx_s, c, meta[2 + c], meta[2 + c])

        return carry

    lax.fori_loop(0, chunks, body, 0)


def run_stage(number, meta, lefts, rights, slots, chunks, state, *after):
    new_left = [(at, start, ref.shape[0]) for at, start, ref in lefts]
    new_right = [(at, start, ref.shape[0]) for at, start, ref in rights]
    operands = [ref for _, _, ref in lefts + rights]
    n = len(operands)
    smem = pl.BlockSpec(memory_space=pltpu.SMEM)
    vmem = pl.BlockSpec(memory_space=pltpu.VMEM)
    far_off = pl.BlockSpec(memory_space=pl.ANY)
    return pl.pallas_call(
        lambda *refs: stage(number, new_left, new_right, slots, chunks, *refs),
        out_shape=[
            jax.ShapeDtypeStruct((8, W, CELL), jnp.float32),
            jax.ShapeDtypeStruct((NY, 2 * LPART, W), jnp.bfloat16),
            jax.ShapeDtypeStruct((NZ, 2 * RPART, W), jnp.bfloat16),
            jax.ShapeDtypeStruct((8, W), jnp.int32),
        ],
        in_specs=[smem] + [far_off] * n + [vmem] * len(state) + [far_off] * len(after),
        out_specs=[vmem] * 4,
        input_output_aliases={1 + n + i: i for i in range(len(state))},
        scratch_shapes=[
            pltpu.VMEM((4 * NY, W), jnp.int32),
            pltpu.SMEM((4 * NY, W), jnp.int32),
            pltpu.SemaphoreType.DMA,
            pltpu.SemaphoreType.DMA((8,)),
        ],
        compiler_params=pltpu.CompilerParams(vmem_limit_bytes=VMEM_LIMIT),
        cost_estimate=pl.CostEstimate(
            flops=8 * 48 * W**3, bytes_accessed=2**20, transcendentals=0
        ),
    )(meta, *operands, *state, *after)


def encode(total):
    top = jnp.maximum(jnp.abs(total).max(axis=-1, keepdims=True), 2.0**-100)
    power = jnp.ceil(jnp.log2(top))
    whole = jnp.round(total * jnp.exp2(-power) * TOP)
    whole = jnp.clip(whole, -TOP, TOP).astype(jnp.int16)
    power = jnp.broadcast_to(power.astype(jnp.int16), total.shape[:-1] + (W,))
    return jnp.concatenate([whole, power], axis=-1)


def decode(moved):
    power = moved[..., CELL : CELL + 1].astype(jnp.float32)
    return moved[..., :CELL].astype(jnp.float32) * (jnp.exp2(power) / TOP)


def per_device(left_blocks, left_rows, right_blocks, right_cols):
    x_lo = lax.axis_index("x_lo")
    z = lax.axis_index("z")
    y = lax.axis_index("y")
    core = lax.axis_index("core")
    side = x_lo ^ zig(z)

    left = left_blocks.reshape(2, GROUP * W, W)
    rows = left_rows.reshape(2, GROUP)
    own = (side + y // 4 + y % 4) % 2

    def group(which):
        return with_index(
            lax.dynamic_index_in_dim(left, which, 0, False),
            lax.dynamic_index_in_dim(rows, which, 0, False),
        )

    swapped = lax.ppermute(group(1 - own), "x_lo", [(0, 1), (1, 0)])
    pair = jnp.concatenate([group(own), swapped], axis=0)
    right = right_blocks.reshape(2, HALF, EB * W, W)
    cols = right_cols.reshape(2, HALF * EB)
    chunk = jnp.concatenate([with_index(right[h], cols[h]) for h in range(2)], axis=0)
    first, _ = lax.optimization_barrier((chunk, swapped))

    source = (z + jnp.array([0, -1, 1, -2, 2, -3, 3, 4], jnp.int32)) % NZ
    away = (4 * (zig(source) ^ side) + source // 2 - y) % NY
    slot = jnp.where(
        away == 0, 0, jnp.where(away == 4, 7, jnp.where(away < 4, 2 * away, 15 - 2 * away))
    )
    right_at = jnp.array([1, 1, 1, 2, 2, 3, 3, 4], jnp.int32)
    left_at = jnp.where(slot < 3, 1, jnp.where(slot < 5, 2, 3))
    x = lax.axis_index("x_hi") * 2 + x_lo
    meta = jnp.concatenate(
        [jnp.stack([core, x_lo]), slot, jnp.maximum(right_at, left_at), x[None]]
    )
    meta = meta.astype(jnp.int32)

    def listed(arrays, low, high):
        return [(i, 0, arrays[i]) for i in range(low, high)]

    row = ("x_lo", "z")

    def step_z(up, down):
        return lax.ppermute(up, row, ring_pairs(1)), lax.ppermute(down, row, ring_pairs(-1))

    def step_y(fore, back):
        return lax.ppermute(fore, "y", turn(1)), lax.ppermute(back, "y", turn(-1))

    rights = [chunk, *step_z(first, first)]
    lefts = [pair, *step_y(pair, pair)]
    rights += step_z(*rights[1:3])
    lefts += step_y(*lefts[1:3])
    *state, token = run_stage(1, meta, listed(lefts, 0, 3), listed(rights, 0, 3), 3, 3, [])
    up, down, token = lax.optimization_barrier((*rights[3:5], token))
    rights += step_z(up, down)
    lefts += step_y(*lefts[3:5])
    *state, token = run_stage(2, meta, listed(lefts, 3, 5), listed(rights, 3, 5), 5, 5, state, token)
    last_left = step_y(lefts[5][:LPART], lefts[6][LPART:])
    up, down, token, *last_left = lax.optimization_barrier((*rights[5:7], token, *last_left))
    last_right = step_z(up[:RPART], down[RPART:])
    ends = [(7, 0, last_left[0]), (7, LPART, last_left[1])]
    *state, _ = run_stage(3, meta, listed(lefts, 5, 7) + ends, listed(rights, 5, 7), 8, 7, state, token)
    ends = [(7, 0, last_right[0]), (7, RPART, last_right[1])]
    acc = run_stage(4, meta, [], ends, 8, 8, state)[0]

    got = lax.ppermute(acc[4:], "core", [(0, 1), (1, 0)])
    total = acc[:4] + got
    out = total[0]
    for step in (2, 1, 3):
        moved = lax.ppermute(encode(total[step]), ("x_lo", "x_hi"), chip_pairs(step))
        out = out + decode(moved)
    return out


def solution(mesh):
    split = jax.sharding.Mesh(
        mesh.devices.reshape(2, NZ, NY, 2, 2), ("x_lo", "z", "y", "x_hi", "core")
    )
    row, depth = ("x_lo", "z"), ("x_hi", "core")
    placed = (
        P(depth, "y", row, None, None, None),
        P(depth, "y", row, None),
        P(depth, row, "y", None, None, None),
        P(depth, row, "y", None),
    )
    return jax.shard_map(
        per_device,
        mesh=split,
        in_specs=placed,
        out_specs=P(row + depth, "y"),
        check_vma=False,
    )
```

```python
import jax
import jax.numpy as jnp
from jax import lax
from jax.experimental import pallas as pl
from jax.experimental.pallas import tpu as pltpu
from jax.sharding import PartitionSpec as P

BR = 4
EB = 3
W = 128
NZ = 8
NY = 8
GROUP = 8
HALF = GROUP // 2
PAD = 16
LPART = GROUP * W + PAD
RPART = HALF * EB * W + PAD
CELL = 6 * W
TOP = 32767.0
VMEM_LIMIT = 8 * 2**20


def zig(z):
    return ((z + 1) // 2) % 2


def ring_pairs(step):
    pairs = []
    for x_lo in range(2):
        for z in range(NZ):
            to = (z + step) % NZ
            pairs.append((x_lo * NZ + z, (x_lo ^ zig(z) ^ zig(to)) * NZ + to))
    return pairs


def turn(step):
    return [(y, (y + step) % NY) for y in range(NY)]


def chip_pairs(step):
    def other(i):
        return (i % 2) * 2 + i // 2

    return [(i, other((other(i) + step) % 4)) for i in range(4)]


def with_index(blocks, index):
    flat = blocks.reshape(-1, W)
    row = jnp.zeros((PAD, W), flat.dtype)
    row = row.at[0, : index.size].set(index.reshape(-1).astype(flat.dtype))
    return jnp.concatenate([flat, row], axis=0)


def load_index(meta, left, right, slots, chunks, idx_v, idx_s, sem):
    core, x_lo = meta[0], meta[1]

    def first(ref_rows):
        return ref_rows.astype(jnp.float32)[0:1].astype(jnp.int32)

    for i, slot in enumerate(slots):
        for p in range(2):
            rho = first(left[slot, pl.ds(p * LPART + GROUP * W, PAD), :])
            tile = x_lo if p == 0 else 1 - x_lo
            ahead = ((rho >> 1) * 2 + tile - meta[18]) & 3
            place = ((rho & 1) ^ core) * 4 + ahead
            idx_v[pl.ds(i * 2 + p, 1), :] = place
    for c in chunks:
        for h in range(2):
            row = first(right[c, pl.ds(h * RPART + HALF * EB * W, PAD), :])
            idx_v[pl.ds(2 * NY + 2 * c + h, 1), :] = row
    copy = pltpu.make_async_copy(idx_v, idx_s, sem)
    copy.start()
    copy.wait()


def add_chunk(left, right, acc, idx_s, c, slot, place):
    for k in range(GROUP):
        half, j = k // HALF, k % HALF
        both = jnp.concatenate(
            [left[slot, pl.ds(p * LPART + k * W, W), :] for p in range(2)], axis=0
        )
        wide = jnp.concatenate(
            [right[c, pl.ds(half * RPART + (j * EB + e) * W, W), :] for e in range(EB)], axis=1
        )
        part = jnp.dot(both, wide, preferred_element_type=jnp.float32)
        for e in range(EB):
            cell = idx_s[2 * NY + 2 * c + half, j * EB + e]
            lanes = pl.ds(pl.multiple_of(cell * W, W), W)
            for p in range(2):
                at = idx_s[place * 2 + p, k]
                acc[at, :, lanes] += part[p * W : (p + 1) * W, e * W : (e + 1) * W]


def stage(number, new_left, new_right, slots, chunks, meta, *refs):
    n, m = len(new_left), len(new_right)
    arrived = refs[: n + m]
    acc, left, right, token, idx_v, idx_s, sem, sems = refs[-8:]
    token[...] = jnp.zeros_like(token)
    targets = [left.at[at, pl.ds(start, size)] for at, start, size in new_left]
    targets += [right.at[at, pl.ds(start, size)] for at, start, size in new_right]
    copies = [
        pltpu.make_async_copy(ref, target, sems.at[i])
        for i, (ref, target) in enumerate(zip(arrived, targets))
    ]
    for copy in copies:
        copy.start()
    if number == 1:
        acc[...] = jnp.zeros_like(acc)
    for copy in copies:
        copy.wait()
    if number == 4:
        load_index(meta, left, right, [meta[9]], [7], idx_v, idx_s, sem)
        add_chunk(left, right, acc, idx_s, 7, meta[9], 0)
        return
    load_index(meta, left, right, range(slots), range(chunks), idx_v, idx_s, sem)

    def body(c, carry):
        @pl.when(meta[10 + c] == number)
        def _():
            add_chunk(left, right, acc, idx_s, c, meta[2 + c], meta[2 + c])

        return carry

    lax.fori_loop(0, chunks, body, 0)


def run_stage(number, meta, lefts, rights, slots, chunks, state, *after):
    new_left = [(at, start, ref.shape[0]) for at, start, ref in lefts]
    new_right = [(at, start, ref.shape[0]) for at, start, ref in rights]
    operands = [ref for _, _, ref in lefts + rights]
    n = len(operands)
    smem = pl.BlockSpec(memory_space=pltpu.SMEM)
    vmem = pl.BlockSpec(memory_space=pltpu.VMEM)
    far_off = pl.BlockSpec(memory_space=pl.ANY)
    return pl.pallas_call(
        lambda *refs: stage(number, new_left, new_right, slots, chunks, *refs),
        out_shape=[
            jax.ShapeDtypeStruct((8, W, CELL), jnp.float32),
            jax.ShapeDtypeStruct((NY, 2 * LPART, W), jnp.bfloat16),
            jax.ShapeDtypeStruct((NZ, 2 * RPART, W), jnp.bfloat16),
            jax.ShapeDtypeStruct((8, W), jnp.int32),
        ],
        in_specs=[smem] + [far_off] * n + [vmem] * len(state) + [far_off] * len(after),
        out_specs=[vmem] * 4,
        input_output_aliases={1 + n + i: i for i in range(len(state))},
        scratch_shapes=[
            pltpu.VMEM((4 * NY, W), jnp.int32),
            pltpu.SMEM((4 * NY, W), jnp.int32),
            pltpu.SemaphoreType.DMA,
            pltpu.SemaphoreType.DMA((8,)),
        ],
        compiler_params=pltpu.CompilerParams(vmem_limit_bytes=VMEM_LIMIT),
        cost_estimate=pl.CostEstimate(
            flops=8 * 48 * W**3, bytes_accessed=2**20, transcendentals=0
        ),
    )(meta, *operands, *state, *after)


def encode(total):
    top = jnp.maximum(jnp.abs(total).max(axis=-1, keepdims=True), 2.0**-100)
    power = jnp.ceil(jnp.log2(top))
    whole = jnp.round(total * jnp.exp2(-power) * TOP)
    whole = jnp.clip(whole, -TOP, TOP).astype(jnp.int16)
    power = jnp.broadcast_to(power.astype(jnp.int16), total.shape[:-1] + (W,))
    return jnp.concatenate([whole, power], axis=-1)


def decode(moved):
    power = moved[..., CELL : CELL + 1].astype(jnp.float32)
    return moved[..., :CELL].astype(jnp.float32) * (jnp.exp2(power) / TOP)


def per_device(left_blocks, left_rows, right_blocks, right_cols):
    x_lo = lax.axis_index("x_lo")
    z = lax.axis_index("z")
    y = lax.axis_index("y")
    core = lax.axis_index("core")
    side = x_lo ^ zig(z)

    left = left_blocks.reshape(2, GROUP * W, W)
    rows = left_rows.reshape(2, GROUP)
    own = (side + y // 4 + y % 4) % 2

    def group(which):
        return with_index(
            lax.dynamic_index_in_dim(left, which, 0, False),
            lax.dynamic_index_in_dim(rows, which, 0, False),
        )

    swapped = lax.ppermute(group(1 - own), "x_lo", [(0, 1), (1, 0)])
    pair = jnp.concatenate([group(own), swapped], axis=0)
    right = right_blocks.reshape(2, HALF, EB * W, W)
    cols = right_cols.reshape(2, HALF * EB)
    chunk = jnp.concatenate([with_index(right[h], cols[h]) for h in range(2)], axis=0)
    first, _ = lax.optimization_barrier((chunk, swapped))

    source = (z + jnp.array([0, -1, 1, -2, 2, -3, 3, 4], jnp.int32)) % NZ
    away = (4 * (zig(source) ^ side) + source // 2 - y) % NY
    slot = jnp.where(
        away == 0, 0, jnp.where(away == 4, 7, jnp.where(away < 4, 2 * away, 15 - 2 * away))
    )
    right_at = jnp.array([1, 1, 1, 2, 2, 3, 3, 4], jnp.int32)
    left_at = jnp.where(slot < 3, 1, jnp.where(slot < 5, 2, 3))
    x = lax.axis_index("x_hi") * 2 + x_lo
    meta = jnp.concatenate(
        [jnp.stack([core, x_lo]), slot, jnp.maximum(right_at, left_at), x[None]]
    )
    meta = meta.astype(jnp.int32)

    def listed(arrays, low, high):
        return [(i, 0, arrays[i]) for i in range(low, high)]

    row = ("x_lo", "z")

    def step_z(up, down):
        return lax.ppermute(up, row, ring_pairs(1)), lax.ppermute(down, row, ring_pairs(-1))

    def step_y(fore, back):
        return lax.ppermute(fore, "y", turn(1)), lax.ppermute(back, "y", turn(-1))

    rights = [chunk, *step_z(first, first)]
    lefts = [pair, *step_y(pair, pair)]
    rights += step_z(*rights[1:3])
    lefts += step_y(*lefts[1:3])
    *state, token = run_stage(1, meta, listed(lefts, 0, 3), listed(rights, 0, 3), 3, 3, [])
    fore, back, token = lax.optimization_barrier((*lefts[3:5], token))
    rights += step_z(*rights[3:5])
    lefts += step_y(fore, back)
    *state, token = run_stage(2, meta, listed(lefts, 3, 5), listed(rights, 3, 5), 5, 5, state, token)
    last_left = step_y(lefts[5][:LPART], lefts[6][LPART:])
    up, down, token, *last_left = lax.optimization_barrier((*rights[5:7], token, *last_left))
    last_right = step_z(up[:RPART], down[RPART:])
    ends = [(7, 0, last_left[0]), (7, LPART, last_left[1])]
    *state, _ = run_stage(3, meta, listed(lefts, 5, 7) + ends, listed(rights, 5, 7), 8, 7, state, token)
    ends = [(7, 0, last_right[0]), (7, RPART, last_right[1])]
    acc = run_stage(4, meta, [], ends, 8, 8, state)[0]

    got = lax.ppermute(acc[4:], "core", [(0, 1), (1, 0)])
    total = acc[:4] + got
    out = total[0]
    for step in (2, 1, 3):
        moved = lax.ppermute(encode(total[step]), ("x_lo", "x_hi"), chip_pairs(step))
        out = out + decode(moved)
    return out


def solution(mesh):
    split = jax.sharding.Mesh(
        mesh.devices.reshape(2, NZ, NY, 2, 2), ("x_lo", "z", "y", "x_hi", "core")
    )
    row, depth = ("x_lo", "z"), ("x_hi", "core")
    placed = (
        P(depth, "y", row, None, None, None),
        P(depth, "y", row, None),
        P(depth, row, "y", None, None, None),
        P(depth, row, "y", None),
    )
    return jax.shard_map(
        per_device,
        mesh=split,
        in_specs=placed,
        out_specs=P(row + depth, "y"),
        check_vma=False,
    )
```

```python
import jax
import jax.numpy as jnp
from jax import lax
from jax.experimental import pallas as pl
from jax.experimental.pallas import tpu as pltpu
from jax.sharding import PartitionSpec as P

BR = 4
EB = 3
W = 128
NZ = 8
NY = 8
GROUP = 8
HALF = GROUP // 2
PAD = 16
LPART = GROUP * W + PAD
RPART = HALF * EB * W + PAD
CELL = 6 * W
TOP = 32767.0
VMEM_LIMIT = 8 * 2**20


def zig(z):
    return ((z + 1) // 2) % 2


def ring_pairs(step):
    pairs = []
    for x_lo in range(2):
        for z in range(NZ):
            to = (z + step) % NZ
            pairs.append((x_lo * NZ + z, (x_lo ^ zig(z) ^ zig(to)) * NZ + to))
    return pairs


def turn(step):
    return [(y, (y + step) % NY) for y in range(NY)]


def chip_pairs(step):
    def other(i):
        return (i % 2) * 2 + i // 2

    return [(i, other((other(i) + step) % 4)) for i in range(4)]


def with_index(blocks, index):
    flat = blocks.reshape(-1, W)
    row = jnp.zeros((PAD, W), flat.dtype)
    row = row.at[0, : index.size].set(index.reshape(-1).astype(flat.dtype))
    return jnp.concatenate([flat, row], axis=0)


def load_index(meta, left, right, slots, chunks, idx_v, idx_s, sem):
    core, x_lo = meta[0], meta[1]

    def first(ref_rows):
        return ref_rows.astype(jnp.float32)[0:1].astype(jnp.int32)

    for i, slot in enumerate(slots):
        for p in range(2):
            rho = first(left[slot, pl.ds(p * LPART + GROUP * W, PAD), :])
            tile = x_lo if p == 0 else 1 - x_lo
            ahead = ((rho >> 1) * 2 + tile - meta[18]) & 3
            place = ((rho & 1) ^ core) * 4 + ahead
            idx_v[pl.ds(i * 2 + p, 1), :] = place
    for c in chunks:
        for h in range(2):
            row = first(right[c, pl.ds(h * RPART + HALF * EB * W, PAD), :])
            idx_v[pl.ds(2 * NY + 2 * c + h, 1), :] = row
    copy = pltpu.make_async_copy(idx_v, idx_s, sem)
    copy.start()
    copy.wait()


def add_chunk(left, right, acc, idx_s, c, slot, place):
    for k in range(GROUP):
        half, j = k // HALF, k % HALF
        both = jnp.concatenate(
            [left[slot, pl.ds(p * LPART + k * W, W), :] for p in range(2)], axis=0
        )
        wide = jnp.concatenate(
            [right[c, pl.ds(half * RPART + (j * EB + e) * W, W), :] for e in range(EB)], axis=1
        )
        part = jnp.dot(both, wide, preferred_element_type=jnp.float32)
        for e in range(EB):
            cell = idx_s[2 * NY + 2 * c + half, j * EB + e]
            lanes = pl.ds(pl.multiple_of(cell * W, W), W)
            for p in range(2):
                at = idx_s[place * 2 + p, k]
                acc[at, :, lanes] += part[p * W : (p + 1) * W, e * W : (e + 1) * W]


def stage(number, new_left, new_right, slots, chunks, meta, *refs):
    n, m = len(new_left), len(new_right)
    arrived = refs[: n + m]
    acc, left, right, token, idx_v, idx_s, sem, sems = refs[-8:]
    token[...] = jnp.zeros_like(token)
    targets = [left.at[at, pl.ds(start, size)] for at, start, size in new_left]
    targets += [right.at[at, pl.ds(start, size)] for at, start, size in new_right]
    copies = [
        pltpu.make_async_copy(ref, target, sems.at[i])
        for i, (ref, target) in enumerate(zip(arrived, targets))
    ]
    for copy in copies:
        copy.start()
    if number == 1:
        acc[...] = jnp.zeros_like(acc)
    for copy in copies:
        copy.wait()
    load_index(meta, left, right, range(slots), range(chunks), idx_v, idx_s, sem)

    def body(c, carry):
        @pl.when(meta[10 + c] == number)
        def _():
            add_chunk(left, right, acc, idx_s, c, meta[2 + c], meta[2 + c])

        return carry

    lax.fori_loop(0, chunks, body, 0)


def run_stage(number, meta, lefts, rights, slots, chunks, state, *after):
    new_left = [(at, start, ref.shape[0]) for at, start, ref in lefts]
    new_right = [(at, start, ref.shape[0]) for at, start, ref in rights]
    operands = [ref for _, _, ref in lefts + rights]
    n = len(operands)
    smem = pl.BlockSpec(memory_space=pltpu.SMEM)
    vmem = pl.BlockSpec(memory_space=pltpu.VMEM)
    far_off = pl.BlockSpec(memory_space=pl.ANY)
    return pl.pallas_call(
        lambda *refs: stage(number, new_left, new_right, slots, chunks, *refs),
        out_shape=[
            jax.ShapeDtypeStruct((8, W, CELL), jnp.float32),
            jax.ShapeDtypeStruct((NY, 2 * LPART, W), jnp.bfloat16),
            jax.ShapeDtypeStruct((NZ, 2 * RPART, W), jnp.bfloat16),
            jax.ShapeDtypeStruct((8, W), jnp.int32),
        ],
        in_specs=[smem] + [far_off] * n + [vmem] * len(state) + [far_off] * len(after),
        out_specs=[vmem] * 4,
        input_output_aliases={1 + n + i: i for i in range(len(state))},
        scratch_shapes=[
            pltpu.VMEM((4 * NY, W), jnp.int32),
            pltpu.SMEM((4 * NY, W), jnp.int32),
            pltpu.SemaphoreType.DMA,
            pltpu.SemaphoreType.DMA((8,)),
        ],
        compiler_params=pltpu.CompilerParams(vmem_limit_bytes=VMEM_LIMIT),
        cost_estimate=pl.CostEstimate(
            flops=8 * 48 * W**3, bytes_accessed=2**20, transcendentals=0
        ),
    )(meta, *operands, *state, *after)


def encode(total):
    top = jnp.maximum(jnp.abs(total).max(axis=-1, keepdims=True), 2.0**-100)
    power = jnp.ceil(jnp.log2(top))
    whole = jnp.round(total * jnp.exp2(-power) * TOP)
    whole = jnp.clip(whole, -TOP, TOP).astype(jnp.int16)
    power = jnp.broadcast_to(power.astype(jnp.int16), total.shape[:-1] + (W,))
    return jnp.concatenate([whole, power], axis=-1)


def decode(moved):
    power = moved[..., CELL : CELL + 1].astype(jnp.float32)
    return moved[..., :CELL].astype(jnp.float32) * (jnp.exp2(power) / TOP)


def per_device(left_blocks, left_rows, right_blocks, right_cols):
    x_lo = lax.axis_index("x_lo")
    z = lax.axis_index("z")
    y = lax.axis_index("y")
    core = lax.axis_index("core")
    side = x_lo ^ zig(z)

    left = left_blocks.reshape(2, GROUP * W, W)
    rows = left_rows.reshape(2, GROUP)
    own = (side + y // 4 + y % 4) % 2

    def group(which):
        return with_index(
            lax.dynamic_index_in_dim(left, which, 0, False),
            lax.dynamic_index_in_dim(rows, which, 0, False),
        )

    swapped = lax.ppermute(group(1 - own), "x_lo", [(0, 1), (1, 0)])
    pair = jnp.concatenate([group(own), swapped], axis=0)
    right = right_blocks.reshape(2, HALF, EB * W, W)
    cols = right_cols.reshape(2, HALF * EB)
    chunk = jnp.concatenate([with_index(right[h], cols[h]) for h in range(2)], axis=0)
    first, _ = lax.optimization_barrier((chunk, swapped))

    source = (z + jnp.array([0, -1, 1, -2, 2, -3, 3, 4], jnp.int32)) % NZ
    away = (4 * (zig(source) ^ side) + source // 2 - y) % NY
    slot = jnp.where(
        away == 0, 0, jnp.where(away == 4, 7, jnp.where(away < 4, 2 * away, 15 - 2 * away))
    )
    right_at = jnp.array([1, 1, 1, 2, 2, 3, 3, 4], jnp.int32)
    left_at = jnp.where(slot < 3, 1, jnp.where(slot < 5, 2, jnp.where(slot < 7, 3, 4)))
    x = lax.axis_index("x_hi") * 2 + x_lo
    meta = jnp.concatenate(
        [jnp.stack([core, x_lo]), slot, jnp.maximum(right_at, left_at), x[None]]
    )
    meta = meta.astype(jnp.int32)

    def listed(arrays, low, high):
        return [(i, 0, arrays[i]) for i in range(low, high)]

    row = ("x_lo", "z")

    def step_z(up, down):
        return lax.ppermute(up, row, ring_pairs(1)), lax.ppermute(down, row, ring_pairs(-1))

    def step_y(fore, back):
        return lax.ppermute(fore, "y", turn(1)), lax.ppermute(back, "y", turn(-1))

    rights = [chunk, *step_z(first, first)]
    lefts = [pair, *step_y(pair, pair)]
    rights += step_z(*rights[1:3])
    lefts += step_y(*lefts[1:3])
    *state, token = run_stage(1, meta, listed(lefts, 0, 3), listed(rights, 0, 3), 3, 3, [])
    up, down, token = lax.optimization_barrier((*rights[3:5], token))
    rights += step_z(up, down)
    lefts += step_y(*lefts[3:5])
    *state, token = run_stage(2, meta, listed(lefts, 3, 5), listed(rights, 3, 5), 5, 5, state, token)
    last_left = step_y(lefts[5][:LPART], lefts[6][LPART:])
    up, down, token = lax.optimization_barrier((*rights[5:7], token))
    last_right = step_z(up[:RPART], down[RPART:])
    *state, _ = run_stage(3, meta, listed(lefts, 5, 7), listed(rights, 5, 7), 7, 7, state, token)
    last = [(7, i * LPART, part) for i, part in enumerate(last_left)]
    ends = [(7, i * RPART, part) for i, part in enumerate(last_right)]
    acc = run_stage(4, meta, last, ends, 8, 8, state)[0]

    got = lax.ppermute(acc[4:], "core", [(0, 1), (1, 0)])
    total = acc[:4] + got
    out = total[0]
    for step in (2, 1, 3):
        moved = lax.ppermute(encode(total[step]), ("x_lo", "x_hi"), chip_pairs(step))
        out = out + decode(moved)
    return out


def solution(mesh):
    split = jax.sharding.Mesh(
        mesh.devices.reshape(2, NZ, NY, 2, 2), ("x_lo", "z", "y", "x_hi", "core")
    )
    row, depth = ("x_lo", "z"), ("x_hi", "core")
    placed = (
        P(depth, "y", row, None, None, None),
        P(depth, "y", row, None),
        P(depth, row, "y", None, None, None),
        P(depth, row, "y", None),
    )
    return jax.shard_map(
        per_device,
        mesh=split,
        in_specs=placed,
        out_specs=P(row + depth, "y"),
        check_vma=False,
    )
```

```python
import jax
import jax.numpy as jnp
from jax import lax
from jax.experimental import pallas as pl
from jax.experimental.pallas import tpu as pltpu
from jax.sharding import PartitionSpec as P

BR = 4
EB = 3
W = 128
NZ = 8
NY = 8
GROUP = 8
HALF = GROUP // 2
PAD = 16
LPART = GROUP * W + PAD
RPART = HALF * EB * W + PAD
CELL = 6 * W
TOP = 32767.0
VMEM_LIMIT = 8 * 2**20


def zig(z):
    return ((z + 1) // 2) % 2


def ring_pairs(step):
    pairs = []
    for x_lo in range(2):
        for z in range(NZ):
            to = (z + step) % NZ
            pairs.append((x_lo * NZ + z, (x_lo ^ zig(z) ^ zig(to)) * NZ + to))
    return pairs


def turn(step):
    return [(y, (y + step) % NY) for y in range(NY)]


def chip_pairs(step):
    def other(i):
        return (i % 2) * 2 + i // 2

    return [(i, other((other(i) + step) % 4)) for i in range(4)]


def with_index(blocks, index):
    flat = blocks.reshape(-1, W)
    row = jnp.zeros((PAD, W), flat.dtype)
    row = row.at[0, : index.size].set(index.reshape(-1).astype(flat.dtype))
    return jnp.concatenate([flat, row], axis=0)


def load_index(meta, left, right, slots, chunks, idx_v, idx_s, sem):
    core, x_lo = meta[0], meta[1]

    def first(ref_rows):
        return ref_rows.astype(jnp.float32)[0:1].astype(jnp.int32)

    for i, slot in enumerate(slots):
        for p in range(2):
            rho = first(left[slot, pl.ds(p * LPART + GROUP * W, PAD), :])
            tile = x_lo if p == 0 else 1 - x_lo
            ahead = ((rho >> 1) * 2 + tile - meta[18]) & 3
            place = ((rho & 1) ^ core) * 4 + ahead
            idx_v[pl.ds(i * 2 + p, 1), :] = place
    for c in chunks:
        for h in range(2):
            row = first(right[c, pl.ds(h * RPART + HALF * EB * W, PAD), :])
            idx_v[pl.ds(2 * NY + 2 * c + h, 1), :] = row
    copy = pltpu.make_async_copy(idx_v, idx_s, sem)
    copy.start()
    copy.wait()


def add_chunk(left, right, acc, idx_s, c, slot, place):
    none = jnp.zeros((W, W), jnp.bfloat16)
    for pair in range(GROUP // 2):
        ks = (2 * pair, 2 * pair + 1)
        both = jnp.concatenate(
            [
                jnp.concatenate(
                    [left[slot, pl.ds(p * LPART + k * W, W), :] for p in range(2)], axis=0
                )
                for k in ks
            ],
            axis=1,
        )
        half = ks[0] // HALF
        for e in range(EB):
            one, two = (
                right[c, pl.ds(half * RPART + ((k % HALF) * EB + e) * W, W), :] for k in ks
            )
            wide = jnp.concatenate(
                [jnp.concatenate([one, none], axis=1), jnp.concatenate([none, two], axis=1)],
                axis=0,
            )
            part = jnp.dot(both, wide, preferred_element_type=jnp.float32)
            for i, k in enumerate(ks):
                cell = idx_s[2 * NY + 2 * c + half, (k % HALF) * EB + e]
                lanes = pl.ds(pl.multiple_of(cell * W, W), W)
                for p in range(2):
                    at = idx_s[place * 2 + p, k]
                    acc[at, :, lanes] += part[p * W : (p + 1) * W, i * W : (i + 1) * W]


def stage(number, new_left, new_right, slots, chunks, meta, *refs):
    n, m = len(new_left), len(new_right)
    arrived = refs[: n + m]
    acc, left, right, token, idx_v, idx_s, sem, sems = refs[-8:]
    token[...] = jnp.zeros_like(token)
    targets = [left.at[at, pl.ds(start, size)] for at, start, size in new_left]
    targets += [right.at[at, pl.ds(start, size)] for at, start, size in new_right]
    copies = [
        pltpu.make_async_copy(ref, target, sems.at[i])
        for i, (ref, target) in enumerate(zip(arrived, targets))
    ]
    for copy in copies:
        copy.start()
    if number == 1:
        acc[...] = jnp.zeros_like(acc)
    for copy in copies:
        copy.wait()
    load_index(meta, left, right, range(slots), range(chunks), idx_v, idx_s, sem)

    def body(c, carry):
        @pl.when(meta[10 + c] == number)
        def _():
            add_chunk(left, right, acc, idx_s, c, meta[2 + c], meta[2 + c])

        return carry

    lax.fori_loop(0, chunks, body, 0)


def run_stage(number, meta, lefts, rights, slots, chunks, state, *after):
    new_left = [(at, start, ref.shape[0]) for at, start, ref in lefts]
    new_right = [(at, start, ref.shape[0]) for at, start, ref in rights]
    operands = [ref for _, _, ref in lefts + rights]
    n = len(operands)
    smem = pl.BlockSpec(memory_space=pltpu.SMEM)
    vmem = pl.BlockSpec(memory_space=pltpu.VMEM)
    far_off = pl.BlockSpec(memory_space=pl.ANY)
    return pl.pallas_call(
        lambda *refs: stage(number, new_left, new_right, slots, chunks, *refs),
        out_shape=[
            jax.ShapeDtypeStruct((8, W, CELL), jnp.float32),
            jax.ShapeDtypeStruct((NY, 2 * LPART, W), jnp.bfloat16),
            jax.ShapeDtypeStruct((NZ, 2 * RPART, W), jnp.bfloat16),
            jax.ShapeDtypeStruct((8, W), jnp.int32),
        ],
        in_specs=[smem] + [far_off] * n + [vmem] * len(state) + [far_off] * len(after),
        out_specs=[vmem] * 4,
        input_output_aliases={1 + n + i: i for i in range(len(state))},
        scratch_shapes=[
            pltpu.VMEM((4 * NY, W), jnp.int32),
            pltpu.SMEM((4 * NY, W), jnp.int32),
            pltpu.SemaphoreType.DMA,
            pltpu.SemaphoreType.DMA((8,)),
        ],
        compiler_params=pltpu.CompilerParams(vmem_limit_bytes=VMEM_LIMIT),
        cost_estimate=pl.CostEstimate(
            flops=8 * 48 * W**3, bytes_accessed=2**20, transcendentals=0
        ),
    )(meta, *operands, *state, *after)


def encode(total):
    top = jnp.maximum(jnp.abs(total).max(axis=-1, keepdims=True), 2.0**-100)
    power = jnp.ceil(jnp.log2(top))
    whole = jnp.round(total * jnp.exp2(-power) * TOP)
    whole = jnp.clip(whole, -TOP, TOP).astype(jnp.int16)
    power = jnp.broadcast_to(power.astype(jnp.int16), total.shape[:-1] + (W,))
    return jnp.concatenate([whole, power], axis=-1)


def decode(moved):
    power = moved[..., CELL : CELL + 1].astype(jnp.float32)
    return moved[..., :CELL].astype(jnp.float32) * (jnp.exp2(power) / TOP)


def per_device(left_blocks, left_rows, right_blocks, right_cols):
    x_lo = lax.axis_index("x_lo")
    z = lax.axis_index("z")
    y = lax.axis_index("y")
    core = lax.axis_index("core")
    side = x_lo ^ zig(z)

    left = left_blocks.reshape(2, GROUP * W, W)
    rows = left_rows.reshape(2, GROUP)
    own = (side + y // 4 + y % 4) % 2

    def group(which):
        return lax.dynamic_index_in_dim(left, which, 0, False)

    def group_index(which):
        picked = lax.dynamic_index_in_dim(rows, which, 0, False).astype(left.dtype)
        return jnp.zeros((PAD, W), left.dtype).at[0, :GROUP].set(picked)

    right = right_blocks.reshape(2, HALF, EB * W, W)
    cols = right_cols.reshape(2, HALF * EB)
    chunk = jnp.concatenate([with_index(right[h], cols[h]) for h in range(2)], axis=0)
    swap = [(0, 1), (1, 0)]
    swapped = lax.ppermute(group(1 - own), "x_lo", swap)
    chunk, other = lax.optimization_barrier((chunk, group_index(1 - own)))
    swapped_index = lax.ppermute(other, "x_lo", swap)
    first, swapped, swapped_index = lax.optimization_barrier((chunk, swapped, swapped_index))
    pair = jnp.concatenate([group(own), group_index(own), swapped, swapped_index], axis=0)

    source = (z + jnp.array([0, -1, 1, -2, 2, -3, 3, 4], jnp.int32)) % NZ
    away = (4 * (zig(source) ^ side) + source // 2 - y) % NY
    slot = jnp.where(
        away == 0, 0, jnp.where(away == 4, 7, jnp.where(away < 4, 2 * away, 15 - 2 * away))
    )
    right_at = jnp.array([1, 1, 1, 2, 2, 3, 3, 4], jnp.int32)
    left_at = jnp.where(slot < 3, 1, jnp.where(slot < 5, 2, jnp.where(slot < 7, 3, 4)))
    x = lax.axis_index("x_hi") * 2 + x_lo
    meta = jnp.concatenate(
        [jnp.stack([core, x_lo]), slot, jnp.maximum(right_at, left_at), x[None]]
    )
    meta = meta.astype(jnp.int32)

    def listed(arrays, low, high):
        return [(i, 0, arrays[i]) for i in range(low, high)]

    row = ("x_lo", "z")

    def step_z(up, down):
        return lax.ppermute(up, row, ring_pairs(1)), lax.ppermute(down, row, ring_pairs(-1))

    def step_y(fore, back):
        return lax.ppermute(fore, "y", turn(1)), lax.ppermute(back, "y", turn(-1))

    rights = [chunk, *step_z(first, first)]
    lefts = [pair, *step_y(pair, pair)]
    rights += step_z(*rights[1:3])
    lefts += step_y(*lefts[1:3])
    *state, token = run_stage(1, meta, listed(lefts, 0, 3), listed(rights, 0, 3), 3, 3, [])
    up, down, token = lax.optimization_barrier((*rights[3:5], token))
    rights += step_z(up, down)
    lefts += step_y(*lefts[3:5])
    *state, token = run_stage(2, meta, listed(lefts, 3, 5), listed(rights, 3, 5), 5, 5, state, token)
    last_left = step_y(lefts[5][:LPART], lefts[6][LPART:])
    up, down, token = lax.optimization_barrier((*rights[5:7], token))
    last_right = step_z(up[:RPART], down[RPART:])
    *state, _ = run_stage(3, meta, listed(lefts, 5, 7), listed(rights, 5, 7), 7, 7, state, token)
    last = [(7, i * LPART, part) for i, part in enumerate(last_left)]
    ends = [(7, i * RPART, part) for i, part in enumerate(last_right)]
    acc = run_stage(4, meta, last, ends, 8, 8, state)[0]

    got = lax.ppermute(acc[4:], "core", [(0, 1), (1, 0)])
    total = acc[:4] + got
    out = total[0]
    for step in (2, 1, 3):
        moved = lax.ppermute(encode(total[step]), ("x_lo", "x_hi"), chip_pairs(step))
        out = out + decode(moved)
    return out


def solution(mesh):
    split = jax.sharding.Mesh(
        mesh.devices.reshape(2, NZ, NY, 2, 2), ("x_lo", "z", "y", "x_hi", "core")
    )
    row, depth = ("x_lo", "z"), ("x_hi", "core")
    placed = (
        P(depth, "y", row, None, None, None),
        P(depth, "y", row, None),
        P(depth, row, "y", None, None, None),
        P(depth, row, "y", None),
    )
    return jax.shard_map(
        per_device,
        mesh=split,
        in_specs=placed,
        out_specs=P(row + depth, "y"),
        check_vma=False,
    )
```

```python
import jax
import jax.numpy as jnp
from jax import lax
from jax.experimental import pallas as pl
from jax.experimental.pallas import tpu as pltpu
from jax.sharding import PartitionSpec as P

BR = 4
EB = 3
W = 128
NZ = 8
NY = 8
GROUP = 8
HALF = GROUP // 2
PAD = 16
LPART = GROUP * W + PAD
RPART = HALF * EB * W + PAD
CELL = 6 * W
TOP = 32767.0
VMEM_LIMIT = 8 * 2**20


def zig(z):
    return ((z + 1) // 2) % 2


def ring_pairs(step):
    pairs = []
    for x_lo in range(2):
        for z in range(NZ):
            to = (z + step) % NZ
            pairs.append((x_lo * NZ + z, (x_lo ^ zig(z) ^ zig(to)) * NZ + to))
    return pairs


def turn(step):
    return [(y, (y + step) % NY) for y in range(NY)]


def chip_pairs(step):
    def other(i):
        return (i % 2) * 2 + i // 2

    return [(i, other((other(i) + step) % 4)) for i in range(4)]


def with_index(blocks, index):
    flat = blocks.reshape(-1, W)
    row = jnp.zeros((PAD, W), flat.dtype)
    row = row.at[0, : index.size].set(index.reshape(-1).astype(flat.dtype))
    return jnp.concatenate([flat, row], axis=0)


def load_index(meta, left, right, slots, chunks, idx_v, idx_s, sem):
    core, x_lo = meta[0], meta[1]

    def first(ref_rows):
        return ref_rows.astype(jnp.float32)[0:1].astype(jnp.int32)

    for i, slot in enumerate(slots):
        for p in range(2):
            rho = first(left[slot, pl.ds(p * LPART + GROUP * W, PAD), :])
            tile = x_lo if p == 0 else 1 - x_lo
            ahead = ((rho >> 1) * 2 + tile - meta[18]) & 3
            place = ((rho & 1) ^ core) * 4 + ahead
            idx_v[pl.ds(i * 2 + p, 1), :] = place
    for c in chunks:
        for h in range(2):
            row = first(right[c, pl.ds(h * RPART + HALF * EB * W, PAD), :])
            idx_v[pl.ds(2 * NY + 2 * c + h, 1), :] = row
    copy = pltpu.make_async_copy(idx_v, idx_s, sem)
    copy.start()
    copy.wait()


def add_chunk(left, right, acc, idx_s, c, slot, place):
    for k in range(GROUP):
        half, j = k // HALF, k % HALF
        both = jnp.concatenate(
            [left[slot, pl.ds(p * LPART + k * W, W), :] for p in range(2)], axis=0
        )
        wide = jnp.concatenate(
            [right[c, pl.ds(half * RPART + (j * EB + e) * W, W), :] for e in range(EB)], axis=1
        )
        part = jnp.dot(both, wide, preferred_element_type=jnp.float32)
        for e in range(EB):
            cell = idx_s[2 * NY + 2 * c + half, j * EB + e]
            lanes = pl.ds(pl.multiple_of(cell * W, W), W)
            for p in range(2):
                at = idx_s[place * 2 + p, k]
                acc[at, :, lanes] += part[p * W : (p + 1) * W, e * W : (e + 1) * W]


def stage(number, new_left, new_right, slots, chunks, meta, *refs):
    n, m = len(new_left), len(new_right)
    arrived = refs[: n + m]
    acc, left, right, token, idx_v, idx_s, sem, sems = refs[-8:]
    token[...] = jnp.zeros_like(token)
    targets = [left.at[at, pl.ds(start, size)] for at, start, size in new_left]
    targets += [right.at[at, pl.ds(start, size)] for at, start, size in new_right]
    copies = [
        pltpu.make_async_copy(ref, target, sems.at[i])
        for i, (ref, target) in enumerate(zip(arrived, targets))
    ]
    for copy in copies:
        copy.start()
    if number == 1:
        acc[...] = jnp.zeros_like(acc)
    for copy in copies:
        copy.wait()
    load_index(meta, left, right, range(slots), range(chunks), idx_v, idx_s, sem)

    def body(c, carry):
        @pl.when(meta[10 + c] == number)
        def _():
            add_chunk(left, right, acc, idx_s, c, meta[2 + c], meta[2 + c])

        return carry

    lax.fori_loop(0, chunks, body, 0)


def run_stage(number, meta, lefts, rights, slots, chunks, state, *after):
    new_left = [(at, start, ref.shape[0]) for at, start, ref in lefts]
    new_right = [(at, start, ref.shape[0]) for at, start, ref in rights]
    operands = [ref for _, _, ref in lefts + rights]
    n = len(operands)
    smem = pl.BlockSpec(memory_space=pltpu.SMEM)
    vmem = pl.BlockSpec(memory_space=pltpu.VMEM)
    far_off = pl.BlockSpec(memory_space=pl.ANY)
    return pl.pallas_call(
        lambda *refs: stage(number, new_left, new_right, slots, chunks, *refs),
        out_shape=[
            jax.ShapeDtypeStruct((8, W, CELL), jnp.float32),
            jax.ShapeDtypeStruct((NY, 2 * LPART, W), jnp.bfloat16),
            jax.ShapeDtypeStruct((NZ, 2 * RPART, W), jnp.bfloat16),
            jax.ShapeDtypeStruct((8, W), jnp.int32),
        ],
        in_specs=[smem] + [far_off] * n + [vmem] * len(state) + [far_off] * len(after),
        out_specs=[vmem] * 4,
        input_output_aliases={1 + n + i: i for i in range(len(state))},
        scratch_shapes=[
            pltpu.VMEM((4 * NY, W), jnp.int32),
            pltpu.SMEM((4 * NY, W), jnp.int32),
            pltpu.SemaphoreType.DMA,
            pltpu.SemaphoreType.DMA((8,)),
        ],
        compiler_params=pltpu.CompilerParams(vmem_limit_bytes=VMEM_LIMIT),
        cost_estimate=pl.CostEstimate(
            flops=8 * 48 * W**3, bytes_accessed=2**20, transcendentals=0
        ),
    )(meta, *operands, *state, *after)


def encode(total):
    top = jnp.maximum(jnp.abs(total).max(axis=-1, keepdims=True), 2.0**-100)
    power = jnp.ceil(jnp.log2(top))
    whole = jnp.round(total * jnp.exp2(-power) * TOP)
    whole = jnp.clip(whole, -TOP, TOP).astype(jnp.int16)
    power = jnp.broadcast_to(power.astype(jnp.int16), total.shape[:-1] + (W,))
    return jnp.concatenate([whole, power], axis=-1)


def decode(moved):
    power = moved[..., CELL : CELL + 1].astype(jnp.float32)
    return moved[..., :CELL].astype(jnp.float32) * (jnp.exp2(power) / TOP)


def per_device(left_blocks, left_rows, right_blocks, right_cols):
    x_lo = lax.axis_index("x_lo")
    z = lax.axis_index("z")
    y = lax.axis_index("y")
    core = lax.axis_index("core")
    side = x_lo ^ zig(z)

    left = left_blocks.reshape(2, GROUP * W, W)
    rows = left_rows.reshape(2, GROUP)
    own = (side + y // 4 + y % 4) % 2

    def group(which):
        return lax.dynamic_index_in_dim(left, which, 0, False)

    def group_index(which):
        picked = lax.dynamic_index_in_dim(rows, which, 0, False).astype(left.dtype)
        return jnp.zeros((PAD, W), left.dtype).at[0, :GROUP].set(picked)

    right = right_blocks.reshape(2, HALF, EB * W, W)
    cols = right_cols.reshape(2, HALF * EB)
    chunk = jnp.concatenate([with_index(right[h], cols[h]) for h in range(2)], axis=0)
    swap = [(0, 1), (1, 0)]
    swapped = lax.ppermute(group(1 - own), "x_lo", swap)
    chunk, other = lax.optimization_barrier((chunk, group_index(1 - own)))
    swapped_index = lax.ppermute(other, "x_lo", swap)
    first, swapped = lax.optimization_barrier((chunk, swapped))
    pair = jnp.concatenate([group(own), group_index(own), swapped, swapped_index], axis=0)

    source = (z + jnp.array([0, -1, 1, -2, 2, -3, 3, 4], jnp.int32)) % NZ
    away = (4 * (zig(source) ^ side) + source // 2 - y) % NY
    slot = jnp.where(
        away == 0, 0, jnp.where(away == 4, 7, jnp.where(away < 4, 2 * away, 15 - 2 * away))
    )
    right_at = jnp.array([1, 1, 1, 2, 2, 3, 3, 4], jnp.int32)
    left_at = jnp.where(slot < 3, 1, jnp.where(slot < 5, 2, jnp.where(slot < 7, 3, 4)))
    x = lax.axis_index("x_hi") * 2 + x_lo
    meta = jnp.concatenate(
        [jnp.stack([core, x_lo]), slot, jnp.maximum(right_at, left_at), x[None]]
    )
    meta = meta.astype(jnp.int32)

    def listed(arrays, low, high):
        return [(i, 0, arrays[i]) for i in range(low, high)]

    row = ("x_lo", "z")

    def step_z(up, down):
        return lax.ppermute(up, row, ring_pairs(1)), lax.ppermute(down, row, ring_pairs(-1))

    def step_y(fore, back):
        return lax.ppermute(fore, "y", turn(1)), lax.ppermute(back, "y", turn(-1))

    rights = [chunk, *step_z(first, first)]
    lefts = [pair, *step_y(pair, pair)]
    rights += step_z(*rights[1:3])
    lefts += step_y(*lefts[1:3])
    *state, token = run_stage(1, meta, listed(lefts, 0, 3), listed(rights, 0, 3), 3, 3, [])
    up, down, token = lax.optimization_barrier((*rights[3:5], token))
    rights += step_z(up, down)
    lefts += step_y(*lefts[3:5])
    *state, token = run_stage(2, meta, listed(lefts, 3, 5), listed(rights, 3, 5), 5, 5, state, token)
    last_left = step_y(lefts[5][:LPART], lefts[6][LPART:])
    up, down, token = lax.optimization_barrier((*rights[5:7], token))
    last_right = step_z(up[:RPART], down[RPART:])
    *state, _ = run_stage(3, meta, listed(lefts, 5, 7), listed(rights, 5, 7), 7, 7, state, token)
    last = [(7, i * LPART, part) for i, part in enumerate(last_left)]
    ends = [(7, i * RPART, part) for i, part in enumerate(last_right)]
    acc = run_stage(4, meta, last, ends, 8, 8, state)[0]

    got = lax.ppermute(acc[4:], "core", [(0, 1), (1, 0)])
    total = acc[:4] + got
    out = total[0]
    for step in (2, 1, 3):
        moved = lax.ppermute(encode(total[step]), ("x_lo", "x_hi"), chip_pairs(step))
        out = out + decode(moved)
    return out


def solution(mesh):
    split = jax.sharding.Mesh(
        mesh.devices.reshape(2, NZ, NY, 2, 2), ("x_lo", "z", "y", "x_hi", "core")
    )
    row, depth = ("x_lo", "z"), ("x_hi", "core")
    placed = (
        P(depth, "y", row, None, None, None),
        P(depth, "y", row, None),
        P(depth, row, "y", None, None, None),
        P(depth, row, "y", None),
    )
    return jax.shard_map(
        per_device,
        mesh=split,
        in_specs=placed,
        out_specs=P(row + depth, "y"),
        check_vma=False,
    )
```

```python
import jax
import jax.numpy as jnp
from jax import lax
from jax.experimental import pallas as pl
from jax.experimental.pallas import tpu as pltpu
from jax.sharding import PartitionSpec as P

BR = 4
EB = 3
W = 128
NZ = 8
NY = 8
GROUP = 8
HALF = GROUP // 2
PAD = 16
LPART = GROUP * W + PAD
RPART = HALF * EB * W + PAD
CELL = 6 * W
BASE = 2 * NY * GROUP
TOP = 32767.0
VMEM_LIMIT = 8 * 2**20


def zig(z):
    return ((z + 1) // 2) % 2


def ring_pairs(step):
    pairs = []
    for x_lo in range(2):
        for z in range(NZ):
            to = (z + step) % NZ
            pairs.append((x_lo * NZ + z, (x_lo ^ zig(z) ^ zig(to)) * NZ + to))
    return pairs


def turn(step):
    return [(y, (y + step) % NY) for y in range(NY)]


def chip_pairs(step):
    def other(i):
        return (i % 2) * 2 + i // 2

    return [(i, other((other(i) + step) % 4)) for i in range(4)]


def with_index(blocks, index):
    flat = blocks.reshape(-1, W)
    row = jnp.zeros((PAD, W), flat.dtype)
    row = row.at[0, : index.size].set(index.reshape(-1).astype(flat.dtype))
    return jnp.concatenate([flat, row], axis=0)


def load_index(meta, left, right, slots, chunks, idx_v, idx_s, sem):
    core, x_lo = meta[0], meta[1]

    def first(ref_rows):
        return ref_rows.astype(jnp.float32)[0:1].astype(jnp.int32)

    for i, slot in enumerate(slots):
        for p in range(2):
            held = left[slot, pl.ds(p * LPART + GROUP * W, PAD), :]
            rho = held.astype(jnp.float32)[0:GROUP].astype(jnp.int32)
            tile = x_lo if p == 0 else 1 - x_lo
            ahead = ((rho >> 1) * 2 + tile - meta[18]) & 3
            place = ((rho & 1) ^ core) * 4 + ahead
            idx_v[pl.ds((slot * 2 + p) * GROUP, GROUP), :] = place
    for c in chunks:
        for h in range(2):
            row = first(right[c, pl.ds(h * RPART + HALF * EB * W, PAD), :])
            idx_v[pl.ds(BASE + 2 * c + h, 1), :] = row
    copy = pltpu.make_async_copy(idx_v, idx_s, sem)
    copy.start()
    copy.wait()


def add_chunk(left, right, acc, idx_s, c, slot, place):
    for k in range(GROUP):
        half, j = k // HALF, k % HALF
        both = jnp.concatenate(
            [left[slot, pl.ds(p * LPART + k * W, W), :] for p in range(2)], axis=0
        )
        wide = jnp.concatenate(
            [right[c, pl.ds(half * RPART + (j * EB + e) * W, W), :] for e in range(EB)], axis=1
        )
        part = jnp.dot(both, wide, preferred_element_type=jnp.float32)
        for e in range(EB):
            cell = idx_s[BASE + 2 * c + half, j * EB + e]
            lanes = pl.ds(pl.multiple_of(cell * W, W), W)
            for p in range(2):
                at = idx_s[(place * 2 + p) * GROUP + k, 0]
                acc[at, :, lanes] += part[p * W : (p + 1) * W, e * W : (e + 1) * W]


def stage(number, new_left, new_right, slots, chunks, meta, *refs):
    n, m = len(new_left), len(new_right)
    arrived = refs[: n + m]
    acc, left, right, token, idx_v, idx_s, sem, sems = refs[-8:]
    token[...] = jnp.zeros_like(token)
    targets = [left.at[at, pl.ds(start, size)] for at, start, size in new_left]
    targets += [right.at[at, pl.ds(start, size)] for at, start, size in new_right]
    copies = [
        pltpu.make_async_copy(ref, target, sems.at[i])
        for i, (ref, target) in enumerate(zip(arrived, targets))
    ]
    for copy in copies:
        copy.start()
    if number == 1:
        acc[...] = jnp.zeros_like(acc)
    for copy in copies:
        copy.wait()
    load_index(meta, left, right, range(slots), range(chunks), idx_v, idx_s, sem)

    def body(c, carry):
        @pl.when(meta[10 + c] == number)
        def _():
            add_chunk(left, right, acc, idx_s, c, meta[2 + c], meta[2 + c])

        return carry

    lax.fori_loop(0, chunks, body, 0)


def run_stage(number, meta, lefts, rights, slots, chunks, state, *after):
    new_left = [(at, start, ref.shape[0]) for at, start, ref in lefts]
    new_right = [(at, start, ref.shape[0]) for at, start, ref in rights]
    operands = [ref for _, _, ref in lefts + rights]
    n = len(operands)
    smem = pl.BlockSpec(memory_space=pltpu.SMEM)
    vmem = pl.BlockSpec(memory_space=pltpu.VMEM)
    far_off = pl.BlockSpec(memory_space=pl.ANY)
    return pl.pallas_call(
        lambda *refs: stage(number, new_left, new_right, slots, chunks, *refs),
        out_shape=[
            jax.ShapeDtypeStruct((8, W, CELL), jnp.float32),
            jax.ShapeDtypeStruct((NY, 2 * LPART, W), jnp.bfloat16),
            jax.ShapeDtypeStruct((NZ, 2 * RPART, W), jnp.bfloat16),
            jax.ShapeDtypeStruct((8, W), jnp.int32),
        ],
        in_specs=[smem] + [far_off] * n + [vmem] * len(state) + [far_off] * len(after),
        out_specs=[vmem] * 4,
        input_output_aliases={1 + n + i: i for i in range(len(state))},
        scratch_shapes=[
            pltpu.VMEM((BASE + 2 * NZ, W), jnp.int32),
            pltpu.SMEM((BASE + 2 * NZ, W), jnp.int32),
            pltpu.SemaphoreType.DMA,
            pltpu.SemaphoreType.DMA((8,)),
        ],
        compiler_params=pltpu.CompilerParams(vmem_limit_bytes=VMEM_LIMIT),
        cost_estimate=pl.CostEstimate(
            flops=8 * 48 * W**3, bytes_accessed=2**20, transcendentals=0
        ),
    )(meta, *operands, *state, *after)


def encode(total):
    top = jnp.maximum(jnp.abs(total).max(axis=-1, keepdims=True), 2.0**-100)
    power = jnp.ceil(jnp.log2(top))
    whole = jnp.round(total * jnp.exp2(-power) * TOP)
    whole = jnp.clip(whole, -TOP, TOP).astype(jnp.int16)
    power = jnp.broadcast_to(power.astype(jnp.int16), total.shape[:-1] + (W,))
    return jnp.concatenate([whole, power], axis=-1)


def decode(moved):
    power = moved[..., CELL : CELL + 1].astype(jnp.float32)
    return moved[..., :CELL].astype(jnp.float32) * (jnp.exp2(power) / TOP)


def per_device(left_blocks, left_rows, right_blocks, right_cols):
    x_lo = lax.axis_index("x_lo")
    z = lax.axis_index("z")
    y = lax.axis_index("y")
    core = lax.axis_index("core")
    side = x_lo ^ zig(z)

    left = left_blocks.reshape(2, GROUP * W, W)
    rows = jnp.broadcast_to(left_rows[0, :, 0, :].astype(left.dtype), (2 * GROUP, W))
    own = (side + y // 4 + y % 4) % 2

    def group(which):
        picked = lax.dynamic_slice_in_dim(rows, which * GROUP, GROUP, 0)
        blocks = lax.dynamic_index_in_dim(left, which, 0, False)
        return jnp.concatenate([blocks, picked, jnp.zeros_like(picked)], axis=0)

    swapped = lax.ppermute(group(1 - own), "x_lo", [(0, 1), (1, 0)])
    pair = jnp.concatenate([group(own), swapped], axis=0)
    right = right_blocks.reshape(2, HALF, EB * W, W)
    cols = right_cols.reshape(2, HALF * EB)
    chunk = jnp.concatenate([with_index(right[h], cols[h]) for h in range(2)], axis=0)
    first, _ = lax.optimization_barrier((chunk, swapped))

    source = (z + jnp.array([0, -1, 1, -2, 2, -3, 3, 4], jnp.int32)) % NZ
    away = (4 * (zig(source) ^ side) + source // 2 - y) % NY
    slot = jnp.where(
        away == 0, 0, jnp.where(away == 4, 7, jnp.where(away < 4, 2 * away, 15 - 2 * away))
    )
    right_at = jnp.array([1, 1, 1, 2, 2, 3, 3, 4], jnp.int32)
    left_at = jnp.where(slot < 3, 1, jnp.where(slot < 5, 2, jnp.where(slot < 7, 3, 4)))
    x = lax.axis_index("x_hi") * 2 + x_lo
    meta = jnp.concatenate(
        [jnp.stack([core, x_lo]), slot, jnp.maximum(right_at, left_at), x[None]]
    )
    meta = meta.astype(jnp.int32)

    def listed(arrays, low, high):
        return [(i, 0, arrays[i]) for i in range(low, high)]

    row = ("x_lo", "z")

    def step_z(up, down):
        return lax.ppermute(up, row, ring_pairs(1)), lax.ppermute(down, row, ring_pairs(-1))

    def step_y(fore, back):
        return lax.ppermute(fore, "y", turn(1)), lax.ppermute(back, "y", turn(-1))

    rights = [chunk, *step_z(first, first)]
    lefts = [pair, *step_y(pair, pair)]
    rights += step_z(*rights[1:3])
    lefts += step_y(*lefts[1:3])
    *state, token = run_stage(1, meta, listed(lefts, 0, 3), listed(rights, 0, 3), 3, 3, [])
    up, down, token = lax.optimization_barrier((*rights[3:5], token))
    rights += step_z(up, down)
    lefts += step_y(*lefts[3:5])
    *state, token = run_stage(2, meta, listed(lefts, 3, 5), listed(rights, 3, 5), 5, 5, state, token)
    last_left = step_y(lefts[5][:LPART], lefts[6][LPART:])
    up, down, token = lax.optimization_barrier((*rights[5:7], token))
    last_right = step_z(up[:RPART], down[RPART:])
    *state, _ = run_stage(3, meta, listed(lefts, 5, 7), listed(rights, 5, 7), 7, 7, state, token)
    last = [(7, i * LPART, part) for i, part in enumerate(last_left)]
    ends = [(7, i * RPART, part) for i, part in enumerate(last_right)]
    acc = run_stage(4, meta, last, ends, 8, 8, state)[0]

    got = lax.ppermute(acc[4:], "core", [(0, 1), (1, 0)])
    total = acc[:4] + got
    out = total[0]
    for step in (2, 1, 3):
        moved = lax.ppermute(encode(total[step]), ("x_lo", "x_hi"), chip_pairs(step))
        out = out + decode(moved)
    return out


def solution(mesh):
    split = jax.sharding.Mesh(
        mesh.devices.reshape(2, NZ, NY, 2, 2), ("x_lo", "z", "y", "x_hi", "core")
    )
    row, depth = ("x_lo", "z"), ("x_hi", "core")
    placed = (
        P(depth, "y", row, None, None, None),
        P(depth, "y", row, None),
        P(depth, row, "y", None, None, None),
        P(depth, row, "y", None),
    )
    return jax.shard_map(
        per_device,
        mesh=split,
        in_specs=placed,
        out_specs=P(row + depth, "y"),
        check_vma=False,
    )
```

```python
import jax
import jax.numpy as jnp
from jax import lax
from jax.experimental import pallas as pl
from jax.experimental.pallas import tpu as pltpu
from jax.sharding import PartitionSpec as P

BR = 4
EB = 3
W = 128
NZ = 8
NY = 8
GROUP = 8
HALF = GROUP // 2
PAD = 16
LPART = GROUP * W + PAD
RPART = HALF * EB * W + PAD
CELL = 6 * W
TOP = 32767.0
VMEM_LIMIT = 8 * 2**20


def zig(z):
    return ((z + 1) // 2) % 2


def ring_pairs(step):
    pairs = []
    for x_lo in range(2):
        for z in range(NZ):
            to = (z + step) % NZ
            pairs.append((x_lo * NZ + z, (x_lo ^ zig(z) ^ zig(to)) * NZ + to))
    return pairs


def turn(step):
    return [(y, (y + step) % NY) for y in range(NY)]


def chip_pairs(step):
    def other(i):
        return (i % 2) * 2 + i // 2

    return [(i, other((other(i) + step) % 4)) for i in range(4)]


def with_index(blocks, index):
    flat = blocks.reshape(-1, W)
    row = jnp.zeros((PAD, W), flat.dtype)
    row = row.at[0, : index.size].set(index.reshape(-1).astype(flat.dtype))
    return jnp.concatenate([flat, row], axis=0)


def load_index(meta, left, right, slots, chunks, idx_v, idx_s, sem):
    core, x_lo = meta[0], meta[1]

    def first(ref_rows):
        return ref_rows.astype(jnp.float32)[0:1].astype(jnp.int32)

    for i, slot in enumerate(slots):
        for p in range(2):
            rho = first(left[slot, pl.ds(p * LPART + GROUP * W, PAD), :])
            tile = x_lo if p == 0 else 1 - x_lo
            ahead = ((rho >> 1) * 2 + tile - meta[18]) & 3
            place = ((rho & 1) ^ core) * 4 + ahead
            idx_v[pl.ds(i * 2 + p, 1), :] = place
    for c in chunks:
        for h in range(2):
            row = first(right[c, pl.ds(h * RPART + HALF * EB * W, PAD), :])
            idx_v[pl.ds(2 * NY + 2 * c + h, 1), :] = row
    copy = pltpu.make_async_copy(idx_v, idx_s, sem)
    copy.start()
    copy.wait()


def add_chunk(left, right, acc, idx_s, c, slot, place):
    for k in range(GROUP):
        half, j = k // HALF, k % HALF
        both = jnp.concatenate(
            [left[slot, pl.ds(p * LPART + k * W, W), :] for p in range(2)], axis=0
        )
        wide = jnp.concatenate(
            [right[c, pl.ds(half * RPART + (j * EB + e) * W, W), :] for e in range(EB)], axis=1
        )
        part = jnp.dot(both, wide, preferred_element_type=jnp.float32)
        for e in range(EB):
            cell = idx_s[2 * NY + 2 * c + half, j * EB + e]
            lanes = pl.ds(pl.multiple_of(cell * W, W), W)
            for p in range(2):
                at = idx_s[place * 2 + p, k]
                acc[at, :, lanes] += part[p * W : (p + 1) * W, e * W : (e + 1) * W]


def stage(number, new_left, new_right, slots, chunks, meta, *refs):
    n, m = len(new_left), len(new_right)
    arrived = refs[: n + m]
    acc, left, right, token, idx_v, idx_s, sem, sems = refs[-8:]
    token[...] = jnp.zeros_like(token)
    targets = [left.at[at, pl.ds(start, size)] for at, start, size in new_left]
    targets += [right.at[at, pl.ds(start, size)] for at, start, size in new_right]
    copies = [
        pltpu.make_async_copy(ref, target, sems.at[i])
        for i, (ref, target) in enumerate(zip(arrived, targets))
    ]
    for copy in copies:
        copy.start()
    if number == 1:
        acc[...] = jnp.zeros_like(acc)
    for copy in copies:
        copy.wait()
    load_index(meta, left, right, range(slots), range(chunks), idx_v, idx_s, sem)

    def body(c, carry):
        @pl.when(meta[10 + c] == number)
        def _():
            add_chunk(left, right, acc, idx_s, c, meta[2 + c], meta[2 + c])

        return carry

    lax.fori_loop(0, chunks, body, 0)


def run_stage(number, meta, lefts, rights, slots, chunks, state, *after):
    new_left = [(at, start, ref.shape[0]) for at, start, ref in lefts]
    new_right = [(at, start, ref.shape[0]) for at, start, ref in rights]
    operands = [ref for _, _, ref in lefts + rights]
    n = len(operands)
    smem = pl.BlockSpec(memory_space=pltpu.SMEM)
    vmem = pl.BlockSpec(memory_space=pltpu.VMEM)
    far_off = pl.BlockSpec(memory_space=pl.ANY)
    return pl.pallas_call(
        lambda *refs: stage(number, new_left, new_right, slots, chunks, *refs),
        out_shape=[
            jax.ShapeDtypeStruct((8, W, CELL), jnp.float32),
            jax.ShapeDtypeStruct((NY, 2 * LPART, W), jnp.bfloat16),
            jax.ShapeDtypeStruct((NZ, 2 * RPART, W), jnp.bfloat16),
            jax.ShapeDtypeStruct((8, W), jnp.int32),
        ],
        in_specs=[smem] + [far_off] * n + [vmem] * len(state) + [far_off] * len(after),
        out_specs=[vmem] * 4,
        input_output_aliases={1 + n + i: i for i in range(len(state))},
        scratch_shapes=[
            pltpu.VMEM((4 * NY, W), jnp.int32),
            pltpu.SMEM((4 * NY, W), jnp.int32),
            pltpu.SemaphoreType.DMA,
            pltpu.SemaphoreType.DMA((8,)),
        ],
        compiler_params=pltpu.CompilerParams(vmem_limit_bytes=VMEM_LIMIT),
        cost_estimate=pl.CostEstimate(
            flops=8 * 48 * W**3, bytes_accessed=2**20, transcendentals=0
        ),
    )(meta, *operands, *state, *after)


def encode(total):
    top = jnp.maximum(jnp.abs(total).max(axis=-1, keepdims=True), 2.0**-100)
    power = jnp.ceil(jnp.log2(top))
    whole = jnp.round(total * jnp.exp2(-power) * TOP)
    whole = jnp.clip(whole, -TOP, TOP).astype(jnp.int16)
    power = jnp.broadcast_to(power.astype(jnp.int16), total.shape[:-1] + (W,))
    return jnp.concatenate([whole, power], axis=-1)


def decode(moved):
    power = moved[..., CELL : CELL + 1].astype(jnp.float32)
    return moved[..., :CELL].astype(jnp.float32) * (jnp.exp2(power) / TOP)


def per_device(left_blocks, left_rows, right_blocks, right_cols):
    x_lo = lax.axis_index("x_lo")
    z = lax.axis_index("z")
    y = lax.axis_index("y")
    core = lax.axis_index("core")
    side = x_lo ^ zig(z)

    left = left_blocks.reshape(2, GROUP * W, W)
    rows = left_rows.reshape(2, GROUP)
    own = (side + y // 4 + y % 4) % 2

    def group(which):
        return lax.dynamic_index_in_dim(left, which, 0, False)

    def group_index(which):
        picked = lax.dynamic_index_in_dim(rows, which, 0, False).astype(left.dtype)
        return jnp.zeros((PAD, W), left.dtype).at[0, :GROUP].set(picked)

    right = right_blocks.reshape(2, HALF, EB * W, W)
    cols = right_cols.reshape(2, HALF * EB)
    chunk = jnp.concatenate([with_index(right[h], cols[h]) for h in range(2)], axis=0)
    swap = [(0, 1), (1, 0)]
    swapped = lax.ppermute(group(1 - own), "x_lo", swap)
    chunk, other = lax.optimization_barrier((chunk, group_index(1 - own)))
    swapped_index = lax.ppermute(other, "x_lo", swap)
    first, swapped = lax.optimization_barrier((chunk, swapped))
    pair = jnp.concatenate([group(own), group_index(own), swapped, swapped_index], axis=0)

    source = (z + jnp.array([0, -1, 1, -2, 2, -3, 3, 4], jnp.int32)) % NZ
    away = (4 * (zig(source) ^ side) + source // 2 - y) % NY
    slot = jnp.where(
        away == 0, 0, jnp.where(away == 4, 7, jnp.where(away < 4, 2 * away, 15 - 2 * away))
    )
    right_at = jnp.array([1, 1, 1, 2, 2, 3, 3, 4], jnp.int32)
    left_at = jnp.where(slot < 3, 1, jnp.where(slot < 5, 2, jnp.where(slot < 7, 3, 4)))
    x = lax.axis_index("x_hi") * 2 + x_lo
    meta = jnp.concatenate(
        [jnp.stack([core, x_lo]), slot, jnp.maximum(right_at, left_at), x[None]]
    )
    meta = meta.astype(jnp.int32)

    def listed(arrays, low, high):
        return [(i, 0, arrays[i]) for i in range(low, high)]

    row = ("x_lo", "z")

    def step_z(up, down):
        return lax.ppermute(up, row, ring_pairs(1)), lax.ppermute(down, row, ring_pairs(-1))

    def step_y(fore, back):
        return lax.ppermute(fore, "y", turn(1)), lax.ppermute(back, "y", turn(-1))

    rights = [chunk, *step_z(first, first)]
    lefts = [pair, *step_y(pair, pair)]
    rights += step_z(*rights[1:3])
    lefts += step_y(*lefts[1:3])
    *state, token = run_stage(1, meta, listed(lefts, 0, 3), listed(rights, 0, 3), 3, 3, [])
    up, down, token = lax.optimization_barrier((*rights[3:5], token))
    rights += step_z(up, down)
    lefts += step_y(*lefts[3:5])
    *state, token = run_stage(2, meta, listed(lefts, 3, 5), listed(rights, 3, 5), 5, 5, state, token)
    last_left = step_y(lefts[5][:LPART], lefts[6][LPART:])
    up, down, token = lax.optimization_barrier((*rights[5:7], token))
    last_right = step_z(up[:RPART], down[RPART:])
    *state, _ = run_stage(3, meta, listed(lefts, 5, 7), listed(rights, 5, 7), 7, 7, state, token)
    last = [(7, i * LPART, part) for i, part in enumerate(last_left)]
    ends = [(7, i * RPART, part) for i, part in enumerate(last_right)]
    acc = run_stage(4, meta, last, ends, 8, 8, state)[0]

    got = lax.ppermute(acc[4:], "core", [(0, 1), (1, 0)])
    total = acc[:4] + got
    out = total[0]
    for step in (1, 2, 3):
        moved = lax.ppermute(encode(total[step]), ("x_lo", "x_hi"), chip_pairs(step))
        out = out + decode(moved)
    return out


def solution(mesh):
    split = jax.sharding.Mesh(
        mesh.devices.reshape(2, NZ, NY, 2, 2), ("x_lo", "z", "y", "x_hi", "core")
    )
    row, depth = ("x_lo", "z"), ("x_hi", "core")
    placed = (
        P(depth, "y", row, None, None, None),
        P(depth, "y", row, None),
        P(depth, row, "y", None, None, None),
        P(depth, row, "y", None),
    )
    return jax.shard_map(
        per_device,
        mesh=split,
        in_specs=placed,
        out_specs=P(row + depth, "y"),
        check_vma=False,
    )
```
